256 devices in a mesh: rep: 32 (over z, y_lo, core), fsdp: 8 (over y_hi, x).
Axes of the slice: x: 4, y: 4 (y_hi: 2, y_lo: 2; y = y_hi * 2 + y_lo), z: 8, core: 2. Of those that a mesh axis runs over, the one named last changes fastest.
Arguments:
- tokens: bfloat16 [32768, 8192], P(('rep', 'fsdp')), may hold values from -6 to 6
- cotangent: bfloat16 [32768, 8192], P(('rep', 'fsdp')), may hold values from -6 to 6
- weights: bfloat16 [32, 8192, 1536], P('rep', 'fsdp'), may hold values from -6 to 6
- global_params: bfloat16 [8192, 1536], P(('fsdp', 'rep')), may hold values from -12 to 12
- momentum: float32 [8192, 1536], P(('fsdp', 'rep')), may hold values from -2 to 2
- fragment: int32 [1], replicated, may hold values from 0 to 65535
Outputs:
- new_weights: bfloat16 [32, 8192, 1536], P('rep', 'fsdp')
- new_global: bfloat16 [8192, 1536], P(('fsdp', 'rep'))
- new_momentum: float32 [8192, 1536], P(('fsdp', 'rep'))
The draws below stay inside these ranges and needn't reach their ends.
All inputs are finite; a program needn't handle non-finite values.
Results may differ from the reference program's by a relative error of at most 0.015.
Values may be sent and summed in bfloat16 or wider, within the bound.
A program may use at most 128 MiB of HBM per device.

```python
import math
import jax
import jax.numpy as jnp
from jax import lax

D = 8192
FRAG = 128
NFRAG = 4
HID = 512
TOK_DEV = 128
TOKENS = 32768
N_REP = 32
N_FSDP = 8


def with_spikes(array, stream_key, source, target, parts, factor):
    def block_of(dim):
        return (jnp.arange(array.shape[dim]) // (array.shape[dim] // parts)).reshape((-1,) + (1,) * (array.ndim - 1 - dim))

    one_side = jax.random.permutation(stream_key, parts)[block_of(target)]
    second = (block_of(target) + parts // 2) % parts
    return jnp.where((block_of(source) == one_side) | (block_of(source) == second), factor * array, array)


def levels(stream_key, shape, shards, least, largest):
    loudness, own = 1.0, jax.random.fold_in(stream_key, 6)
    for axis_at, blocks in shards:
        steps = jnp.exp(jax.random.uniform(jax.random.fold_in(own, axis_at), (blocks,), jnp.float32, least / len(shards), largest / len(shards)))
        loudness = loudness * jnp.repeat(steps, shape[axis_at] // blocks).reshape([-1 if axis == axis_at else 1 for axis in range(len(shape))])
    return loudness


def noise(rng, shape, scale, limit, shards=(), kind=jnp.bfloat16):
    values = scale * jax.random.normal(rng, shape, jnp.float32)
    if shards:
        values = values * levels(rng, shape, shards, -0.22, 0.18)
    return jnp.clip(values, -limit, limit).astype(kind)


def heavy_noise(stream_key, shape, deviation, limit, split, heavy, held_as=jnp.bfloat16):
    drawn = deviation * jax.random.normal(stream_key, shape, jnp.float32)
    if split:
        drawn = drawn * levels(stream_key, shape, split, -0.22, 0.18)
    return jnp.clip(with_spikes(drawn, jax.random.fold_in(stream_key, 3), *heavy), -limit, limit).astype(held_as)


def setup_inputs(seed: int = 0) -> dict:
    arg_keys = jax.random.split(jax.random.key(seed), 7)
    tokens = noise(arg_keys[0], (TOKENS, D), 1.0, 6.0, ((0, 256),))
    cotangent = noise(arg_keys[1], (TOKENS, D), 1.0, 6.0, ((0, 256),))
    weights = heavy_noise(arg_keys[2], (N_REP, D, 3 * HID), 1.0, 6.0, ((0, 32), (1, 8)), (0, 1, 32, 2.75))
    global_params = noise(arg_keys[3], (D, 3 * HID), 2.0, 12.0, ((0, 256),))
    momentum = noise(arg_keys[4], (D, 3 * HID), 0.3, 2.0, ((0, 256),), jnp.float32)
    fragment = jax.random.randint(arg_keys[5], (1,), 0, 65536).astype(jnp.int32)
    return dict(tokens=tokens, cotangent=cotangent, weights=weights, global_params=global_params, momentum=momentum, fragment=fragment)


INNER_RATE = 0.5
OUTER_RATE = 0.7
MOMENT = 0.9
MIX_RATE = 0.5

def take_fragment(source, first_col, hidden_units, frag_width):
    return jnp.concatenate([lax.dynamic_slice_in_dim(source, first_col + member * hidden_units, frag_width, source.ndim - 1) for member in range(3)], axis=-1)

def place_fragment(source, first_col, hidden_units, frag_width, values_in):
    for member in range(3):
        source = lax.dynamic_update_slice_in_dim(source, values_in[..., member * frag_width:(member + 1) * frag_width], first_col + member * hidden_units, source.ndim - 1)
    return source

def device_term(rows_in, grads_in, replica_weights):
    scale_in = 1.0 / math.sqrt(D)
    scale_hid = 1.0 / math.sqrt(HID)
    gate_up = jnp.dot(rows_in, replica_weights[:, :2 * HID], preferred_element_type=jnp.float32) * scale_in
    gate_act = gate_up[:, :HID]
    up_act = gate_up[:, HID:]
    sigmoid_gate = jax.nn.sigmoid(gate_act)
    silu_gate = gate_act * sigmoid_gate
    hidden = (silu_gate * up_act).astype(jnp.bfloat16)
    hidden_grad = jnp.dot(grads_in, replica_weights[:, 2 * HID:], preferred_element_type=jnp.float32) * scale_hid
    dgate = (hidden_grad * up_act * sigmoid_gate * (1.0 + gate_act * (1.0 - sigmoid_gate))).astype(jnp.bfloat16)
    dup = (hidden_grad * silu_gate).astype(jnp.bfloat16)
    paired = jnp.concatenate([dgate, dup], axis=1)
    grad_in = lax.dot_general(rows_in, paired, (((0,), (0,)), ((), ())), preferred_element_type=jnp.float32) * scale_in
    grad_down = lax.dot_general(grads_in, hidden, (((0,), (0,)), ((), ())), preferred_element_type=jnp.float32) * scale_hid
    return jnp.concatenate([grad_in, grad_down], axis=1)

def reference(tokens, cotangent, weights, global_params, momentum, fragment):
    first_col = (fragment[0] % NFRAG).astype(jnp.int32) * FRAG
    rows_all = tokens.reshape(N_REP, N_FSDP, TOK_DEV, D)
    grads_all = cotangent.reshape(N_REP, N_FSDP, TOK_DEV, D)

    def one_replica(replica_item):
        rows_rep, grads_rep, replica_weights = replica_item

        def add_device(running, device_pair):
            partial_term = lax.optimization_barrier(device_term(device_pair[0], device_pair[1], replica_weights).astype(jnp.bfloat16))
            return (running + partial_term.astype(jnp.float32), None)
        gradient, _ = lax.scan(add_device, jnp.zeros((D, 3 * HID), jnp.float32), (rows_rep, grads_rep))
        return (replica_weights.astype(jnp.float32) - INNER_RATE * gradient).astype(jnp.bfloat16)
    updated = lax.map(one_replica, (rows_all, grads_all, weights))
    frag_weights = take_fragment(updated, first_col, HID, FRAG)
    replica_total = lax.optimization_barrier(jnp.sum(frag_weights.astype(jnp.float32), axis=0))
    global_frag = take_fragment(global_params, first_col, HID, FRAG).astype(jnp.float32)
    moment_frag = take_fragment(momentum, first_col, HID, FRAG)
    average = global_frag - replica_total / N_REP
    moment_next = MOMENT * moment_frag + average
    global_next = (global_frag - OUTER_RATE * (average + MOMENT * moment_next)).astype(jnp.bfloat16)
    mixed_rows = (MIX_RATE * frag_weights.astype(jnp.float32) + (1.0 - MIX_RATE) * global_next.astype(jnp.float32)[None]).astype(jnp.bfloat16)
    new_weights = place_fragment(updated, first_col, HID, FRAG, mixed_rows)
    new_global = place_fragment(global_params, first_col, HID, FRAG, global_next)
    new_momentum = place_fragment(momentum, first_col, HID, FRAG, moment_next)
    return (new_weights, new_global, new_momentum)
```

```python
import math

import jax
import jax.numpy as jnp
from jax import lax
from jax.sharding import PartitionSpec as P

D = 8192
FRAG = 128
NFRAG = 4
HID = 512


INNER_RATE = 0.5
OUTER_RATE = 0.7
MOMENT = 0.9
MIX_RATE = 0.5


def take_fragment(source, first_col, hidden_units, frag_width):
    return jnp.concatenate(
        [
            lax.dynamic_slice_in_dim(
                source, first_col + member * hidden_units, frag_width, source.ndim - 1
            )
            for member in range(3)
        ],
        axis=-1,
    )


def place_fragment(source, first_col, hidden_units, frag_width, values_in):
    for member in range(3):
        source = lax.dynamic_update_slice_in_dim(
            source,
            values_in[..., member * frag_width : (member + 1) * frag_width],
            first_col + member * hidden_units,
            source.ndim - 1,
        )
    return source


def shards(tokens, cotangent, weights, global_params, momentum, fragment):
    own_weights = weights[0]
    rows, width = tokens.shape
    n_fsdp = lax.axis_size("fsdp")
    depth = own_weights.shape[0]
    scale_in = 1.0 / math.sqrt(D)
    scale_hid = 1.0 / math.sqrt(HID)
    both = jnp.stack([tokens, cotangent]).reshape(2, rows, n_fsdp, depth)
    both = lax.all_to_all(both.transpose(2, 0, 1, 3), "fsdp", 0, 0, tiled=True)
    tokens_cut = both[:, 0].reshape(n_fsdp * rows, depth)
    cotangent_cut = both[:, 1].reshape(n_fsdp * rows, depth)
    gate_up = jnp.dot(tokens_cut, own_weights[:, : 2 * HID], preferred_element_type=jnp.float32)
    hidden_grad = jnp.dot(
        cotangent_cut, own_weights[:, 2 * HID :], preferred_element_type=jnp.float32
    )
    terms = jnp.concatenate([gate_up * scale_in, hidden_grad * scale_hid], axis=1)
    terms = terms.astype(jnp.bfloat16).reshape(n_fsdp, rows, 3 * HID)
    terms = lax.all_to_all(terms, "fsdp", 0, 0, tiled=True)
    total = jnp.sum(terms.astype(jnp.float32), axis=0)
    gate_act = total[:, :HID]
    up_act = total[:, HID : 2 * HID]
    hidden_grad = total[:, 2 * HID :]
    sigmoid_gate = jax.nn.sigmoid(gate_act)
    silu_gate = gate_act * sigmoid_gate
    hidden = (silu_gate * up_act).astype(jnp.bfloat16)
    dgate = (hidden_grad * up_act * sigmoid_gate * (1.0 + gate_act * (1.0 - sigmoid_gate))).astype(
        jnp.bfloat16
    )
    dup = (hidden_grad * silu_gate).astype(jnp.bfloat16)
    acts = lax.all_gather(
        jnp.concatenate([dgate, dup, hidden], axis=1), "fsdp", axis=0, tiled=True
    )
    over_rows = (((0,), (0,)), ((), ()))
    grad_in = lax.dot_general(
        tokens_cut, acts[:, : 2 * HID], over_rows, preferred_element_type=jnp.float32
    )
    grad_down = lax.dot_general(
        cotangent_cut, acts[:, 2 * HID :], over_rows, preferred_element_type=jnp.float32
    )
    gradient = jnp.concatenate([grad_in * scale_in, grad_down * scale_hid], axis=1)
    updated = (own_weights.astype(jnp.float32) - INNER_RATE * gradient).astype(jnp.bfloat16)
    first_col = fragment[0] % NFRAG * FRAG
    frag_weights = take_fragment(updated, first_col, HID, FRAG)
    global_frag = take_fragment(global_params, first_col, HID, FRAG).astype(jnp.float32)
    moment_frag = take_fragment(momentum, first_col, HID, FRAG)
    replicas = lax.axis_size("rep")
    replica_total = lax.psum_scatter(
        frag_weights, "rep", scatter_dimension=0, tiled=True
    ).astype(jnp.float32)
    average = global_frag - replica_total / replicas
    moment_next = MOMENT * moment_frag + average
    global_next = (global_frag - OUTER_RATE * (average + MOMENT * moment_next)).astype(jnp.bfloat16)
    global_rows = lax.all_gather(global_next, "rep", axis=0, tiled=True)
    mixed_rows = (
        MIX_RATE * frag_weights.astype(jnp.float32)
        + (1.0 - MIX_RATE) * global_rows.astype(jnp.float32)
    ).astype(jnp.bfloat16)
    new_weights = place_fragment(updated, first_col, HID, FRAG, mixed_rows)[None]
    new_global = place_fragment(global_params, first_col, HID, FRAG, global_next)
    new_momentum = place_fragment(momentum, first_col, HID, FRAG, moment_next)
    return (new_weights, new_global, new_momentum)


def solution(mesh):
    placed = (
        P(("rep", "fsdp"), None),
        P(("rep", "fsdp"), None),
        P("rep", "fsdp", None),
        P(("fsdp", "rep"), None),
        P(("fsdp", "rep"), None),
        P(),
    )
    return jax.shard_map(
        shards,
        mesh=mesh,
        in_specs=placed,
        out_specs=(P("rep", "fsdp", None), P(("fsdp", "rep"), None), P(("fsdp", "rep"), None)),
        check_vma=False,
    )
```

```python
import math

import jax
import jax.numpy as jnp
from jax import lax
from jax.experimental import pallas as pl
from jax.experimental.pallas import tpu as pltpu
from jax.sharding import PartitionSpec as P

D = 8192
FRAG = 128
NFRAG = 4
HID = 512
NF = 8
NX = 4
NZ = 8
NQ = 16
ROWS = 128
DEPTH = D // NF
SHARE = 32
WIDE = 3 * FRAG
PAIR = 2 * FRAG
CHUNKS = 2
TILE = 256


INNER_RATE = 0.5
OUTER_RATE = 0.7
MOMENT = 0.9
MIX_RATE = 0.5
SCALE_IN = 1.0 / math.sqrt(D)
SCALE_HID = 1.0 / math.sqrt(HID)
BF16 = jnp.bfloat16
F32 = jnp.float32
MESH = pl.DeviceIdType.MESH


def dot(a, b):
    return jnp.dot(a, b, preferred_element_type=F32)


def step_kernel(
    tokens,
    cotangent,
    weights,
    global_ref,
    moment_ref,
    fragment,
    u_out,
    g_out,
    m_out,
    tcut,
    ccut,
    tturn,
    cturn,
    w,
    wrot,
    ysend,
    yrecv,
    acts,
    u,
    u0,
    r1,
    s1,
    r2,
    gall,
    local_sem,
    a_send,
    a_recv,
    y_send,
    y_recv,
    h_send,
    h_recv,
    c_send,
    c_recv,
    s_send,
    s_recv,
    g_send,
    g_recv,
):
    rep = lax.axis_index("rep")
    me = lax.axis_index("fsdp")
    x, yh = me % NX, me // NX
    core, q = rep % 2, rep // 2
    z, yl = q // 2, q % 2
    frag = lax.rem(fragment[0], NFRAG)

    def fsdp_to(k):
        return (x + k % NX) % NX + NX * ((yh + k // NX) % 2)

    def fsdp_from(k):
        return (x + NX - k % NX) % NX + NX * ((yh + k // NX) % 2)

    def q_to(k):
        return ((z + k // 2) % NZ) * 2 + (yl + k % 2) % 2

    def q_from(k):
        return ((z + NZ - k // 2) % NZ) * 2 + (yl + k % 2) % 2

    def at_fsdp(f):
        return (rep, f)

    def at_q(p):
        return (p * 2 + core, me)

    partner = (q * 2 + 1 - core, me)

    def each(n, body):
        def step(k, carry):
            body(k)
            return carry

        lax.fori_loop(0, n, step, 0)

    barrier = pltpu.get_barrier_semaphore()

    def greet_fsdp(i):
        pl.semaphore_signal(barrier, inc=1, device_id=at_fsdp(fsdp_to(i + 1)), device_id_type=MESH)

    def greet_q(i):
        pl.semaphore_signal(barrier, inc=1, device_id=at_q(q_to(i + 1)), device_id_type=MESH)

    each(NF - 1, greet_fsdp)
    each(NQ - 1, greet_q)
    pl.semaphore_signal(barrier, inc=1, device_id=partner, device_id_type=MESH)

    own_cols = pl.ds(pl.multiple_of(me * DEPTH, DEPTH), DEPTH)
    own_rows = pl.ds(pl.multiple_of(me * ROWS, ROWS), ROWS)
    load_w = pltpu.make_async_copy(weights.at[0], w, local_sem.at[0])
    load_t = pltpu.make_async_copy(tokens.at[:, own_cols], tcut.at[own_rows], local_sem.at[1])
    load_c = pltpu.make_async_copy(cotangent.at[:, own_cols], ccut.at[own_rows], local_sem.at[2])
    load_w.start()
    load_t.start()
    load_c.start()
    pl.semaphore_wait(barrier, NF - 1 + NQ - 1 + 1)

    part = ROWS // CHUNKS

    def exchange(source, target, h, slot, k):
        f = fsdp_to(k)
        cols = pl.ds(pl.multiple_of(f * DEPTH, DEPTH), DEPTH)
        rows = pl.ds(pl.multiple_of(me * ROWS + h * part, part), part)
        return pltpu.make_async_remote_copy(
            src_ref=source.at[pl.ds(h * part, part), cols],
            dst_ref=target.at[rows],
            send_sem=a_send.at[slot, k - 1],
            recv_sem=a_recv.at[slot, k - 1],
            device_id=at_fsdp(f),
            device_id_type=MESH,
        )

    for h in range(CHUNKS):
        each(NF - 1, lambda i: exchange(tokens, tcut, h, h, i + 1).start())
    for h in range(CHUNKS):
        each(NF - 1, lambda i: exchange(cotangent, ccut, h, CHUNKS + h, i + 1).start())

    load_w.wait()
    for j in range(NFRAG):
        first = lax.rem(frag + j, NFRAG) * FRAG
        for member in range(3):
            cols = pl.ds(first + member * HID, FRAG)
            wrot[j, :, member * FRAG : (member + 1) * FRAG] = w[:, cols]

    def tile_of(i):
        return pl.ds(pl.multiple_of(i * TILE, TILE), TILE)

    def spread(j, i, cols, value):
        block = value.astype(BF16).reshape(TILE // ROWS, ROWS, value.shape[-1])
        ysend[j, pl.ds(i * (TILE // ROWS), TILE // ROWS), :, cols] = block

    load_t.wait()
    for h in range(CHUNKS):
        each(NF - 1, lambda i: exchange(tokens, tcut, h, h, i + 1).wait_recv())

    def forward_t(i):
        rows = tcut[tile_of(i), :]
        for j in range(NFRAG):
            spread(j, i, slice(0, PAIR), dot(rows, wrot[j, :, :PAIR]) * SCALE_IN)
        tturn[:, tile_of(i)] = rows.T

    each(NF * ROWS // TILE, forward_t)

    load_c.wait()
    for h in range(CHUNKS):
        each(NF - 1, lambda i: exchange(cotangent, ccut, h, CHUNKS + h, i + 1).wait_recv())

    def forward_c(groups):
        def run(i):
            rows = ccut[tile_of(i), :]
            for j in groups:
                spread(j, i, slice(PAIR, WIDE), dot(rows, wrot[j, :, PAIR:]) * SCALE_HID)

        return run

    def send_terms(first, count, slot, k):
        f = fsdp_to(k)
        return pltpu.make_async_remote_copy(
            src_ref=ysend.at[pl.ds(first, count), f],
            dst_ref=yrecv.at[pl.ds(first, count), k],
            send_sem=y_send.at[slot, k - 1],
            recv_sem=y_recv.at[slot, k - 1],
            device_id=at_fsdp(f),
            device_id_type=MESH,
        )

    def send_acts(first, count, slot, k):
        block = acts.at[pl.ds(first, count), own_rows]
        return pltpu.make_async_remote_copy(
            src_ref=block,
            dst_ref=block,
            send_sem=h_send.at[slot, k - 1],
            recv_sem=h_recv.at[slot, k - 1],
            device_id=at_fsdp(fsdp_to(k)),
            device_id_type=MESH,
        )

    def got_acts(first, count, slot, k):
        block = acts.at[
            pl.ds(first, count), pl.ds(pl.multiple_of(fsdp_from(k) * ROWS, ROWS), ROWS)
        ]
        return pltpu.make_async_remote_copy(
            src_ref=block,
            dst_ref=block,
            send_sem=h_send.at[slot, k - 1],
            recv_sem=h_recv.at[slot, k - 1],
            device_id=at_fsdp(fsdp_to(k)),
            device_id_type=MESH,
        )

    tiles = NF * ROWS // TILE
    each(tiles, forward_c((0,)))
    each(NF - 1, lambda i: send_terms(0, 1, 0, i + 1).start())
    each(tiles, forward_c((1, 2, 3)))
    each(NF - 1, lambda i: send_terms(1, 3, 1, i + 1).start())

    def turn_c(i):
        cturn[:, tile_of(i)] = ccut[tile_of(i), :].T

    each(tiles, turn_c)

    def activate(j):
        total = ysend[j, me].astype(F32)
        for k in range(1, NF):
            total = total + yrecv[j, k].astype(F32)
        gate = total[:, :FRAG]
        up = total[:, FRAG:PAIR]
        hidden_grad = total[:, PAIR:]
        sigmoid = jax.nn.sigmoid(gate)
        silu = gate * sigmoid
        acts[j, own_rows, :FRAG] = (
            hidden_grad * up * sigmoid * (1.0 + gate * (1.0 - sigmoid))
        ).astype(BF16)
        acts[j, own_rows, FRAG:PAIR] = (hidden_grad * silu).astype(BF16)
        acts[j, own_rows, PAIR:] = (silu * up).astype(BF16)

    def descend(j, i):
        rows = tile_of(i)
        grad_in = dot(tturn[rows, :], acts[j, :, :PAIR]) * SCALE_IN
        grad_down = dot(cturn[rows, :], acts[j, :, PAIR:]) * SCALE_HID
        left = wrot[j, rows, :PAIR].astype(F32) - INNER_RATE * grad_in
        right = wrot[j, rows, PAIR:].astype(F32) - INNER_RATE * grad_down
        return left.astype(BF16), right.astype(BF16)

    each(NF - 1, lambda i: send_terms(0, 1, 0, i + 1).wait_recv())
    activate(0)
    each(NF - 1, lambda i: send_acts(0, 1, 0, i + 1).start())
    each(NF - 1, lambda i: got_acts(0, 1, 0, i + 1).wait_recv())

    span = TILE // (2 * SHARE)

    def descend_first(i):
        left, right = descend(0, i)
        at = pl.ds(i * span, span)
        u0[at, :, :, :PAIR] = left.reshape(span, 2, SHARE, PAIR)
        u0[at, :, :, PAIR:] = right.reshape(span, 2, SHARE, FRAG)

    each(DEPTH // TILE, descend_first)

    across = pltpu.make_async_remote_copy(
        src_ref=u0.at[:, 1 - core],
        dst_ref=r1,
        send_sem=c_send.at[0],
        recv_sem=c_recv.at[0],
        device_id=partner,
        device_id_type=MESH,
    )
    across.start()

    each(NF - 1, lambda i: send_terms(1, 3, 1, i + 1).wait_recv())
    for j in range(1, NFRAG):
        activate(j)
    each(NF - 1, lambda i: send_acts(1, 3, 1, i + 1).start())

    across.wait()
    s1[...] = (u0[:, core].astype(F32) + r1[...].astype(F32)).astype(BF16)

    def send_sum(k):
        p = q_to(k)
        return pltpu.make_async_remote_copy(
            src_ref=s1.at[p],
            dst_ref=r2.at[k],
            send_sem=s_send.at[k - 1],
            recv_sem=s_recv.at[k - 1],
            device_id=at_q(p),
            device_id_type=MESH,
        )

    each(NQ - 1, lambda i: send_sum(i + 1).start())
    each(NQ - 1, lambda i: send_sum(i + 1).wait_recv())

    total = s1[q].astype(F32)
    for k in range(1, NQ):
        total = total + r2[k].astype(F32)
    first = frag * FRAG
    for member in range(3):
        cols = pl.ds(first + member * HID, FRAG)
        lanes = slice(member * FRAG, (member + 1) * FRAG)
        old = global_ref[:, cols].astype(F32)
        average = old - total[:, lanes] / (2 * NQ)
        moment = MOMENT * moment_ref[:, cols] + average
        m_out[:, lanes] = moment
        gall[q, core, :, lanes] = (old - OUTER_RATE * (average + MOMENT * moment)).astype(BF16)
    g_out[...] = gall[q, core]

    def send_global(k):
        block = gall.at[q, core]
        return pltpu.make_async_remote_copy(
            src_ref=block,
            dst_ref=block,
            send_sem=g_send.at[k - 1],
            recv_sem=g_recv.at[k - 1],
            device_id=at_q(q_to(k)),
            device_id_type=MESH,
        )

    def got_global(k):
        block = gall.at[q_from(k), core]
        return pltpu.make_async_remote_copy(
            src_ref=block,
            dst_ref=block,
            send_sem=g_send.at[k - 1],
            recv_sem=g_recv.at[k - 1],
            device_id=at_q(q_to(k)),
            device_id_type=MESH,
        )

    each(NQ - 1, lambda i: send_global(i + 1).start())

    each(NF - 1, lambda i: got_acts(1, 3, 1, i + 1).wait_recv())

    def descend_rest(i):
        for j in range(1, NFRAG):
            left, right = descend(j, i)
            u[j, tile_of(i), :PAIR] = left
            u[j, tile_of(i), PAIR:] = right

    each(DEPTH // TILE, descend_rest)
    store_rest = pltpu.make_async_copy(
        u.at[pl.ds(1, 3)], u_out.at[pl.ds(1, 3)], local_sem.at[3]
    )
    store_rest.start()

    each(NQ - 1, lambda i: got_global(i + 1).wait_recv())
    side = gall.at[:, core]
    give = pltpu.make_async_remote_copy(
        src_ref=side,
        dst_ref=side,
        send_sem=c_send.at[1],
        recv_sem=c_recv.at[1],
        device_id=partner,
        device_id_type=MESH,
    )
    give.start()

    for h in range(CHUNKS):
        each(NF - 1, lambda i: exchange(tokens, tcut, h, h, i + 1).wait_send())
        each(NF - 1, lambda i: exchange(cotangent, ccut, h, CHUNKS + h, i + 1).wait_send())
    each(NF - 1, lambda i: send_terms(0, 1, 0, i + 1).wait_send())
    each(NF - 1, lambda i: send_terms(1, 3, 1, i + 1).wait_send())
    each(NF - 1, lambda i: send_acts(0, 1, 0, i + 1).wait_send())
    each(NF - 1, lambda i: send_acts(1, 3, 1, i + 1).wait_send())
    each(NQ - 1, lambda i: send_sum(i + 1).wait_send())
    each(NQ - 1, lambda i: send_global(i + 1).wait_send())

    give.wait_send()
    other = gall.at[:, 1 - core]
    pltpu.make_async_remote_copy(
        src_ref=other,
        dst_ref=other,
        send_sem=c_send.at[1],
        recv_sem=c_recv.at[1],
        device_id=partner,
        device_id_type=MESH,
    ).wait_recv()

    def mix(i):
        at = pl.ds(i * span, span)
        mixed = MIX_RATE * u0[at].astype(F32) + (1.0 - MIX_RATE) * gall[at].astype(F32)
        u[0, tile_of(i), :] = mixed.astype(BF16).reshape(TILE, WIDE)

    each(DEPTH // TILE, mix)
    store_first = pltpu.make_async_copy(u.at[0], u_out.at[0], local_sem.at[4])
    store_first.start()
    store_first.wait()
    store_rest.wait()


def place_kernel(u, g, m, global_ref, moment_ref, fragment, w_out, g_out, m_out, sems):
    frag = jnp.bitwise_and(fragment[0], NFRAG - 1)
    copies = []
    for at in range(NFRAG):
        j = jnp.bitwise_and(at + NFRAG - frag, NFRAG - 1)
        for member in range(3):
            copy = pltpu.make_async_copy(
                u.at[j, :, pl.ds(member * FRAG, FRAG)],
                w_out.at[0, :, pl.ds(member * HID + at * FRAG, FRAG)],
                sems.at[at * 3 + member],
            )
            copy.start()
            copies.append(copy)
    for at in range(NFRAG):
        here = frag == at
        for member in range(3):
            cols = slice(member * HID + at * FRAG, member * HID + (at + 1) * FRAG)
            lanes = slice(member * FRAG, (member + 1) * FRAG)
            g_out[:, cols] = jnp.where(here, g[:, lanes], global_ref[:, cols])
            m_out[:, cols] = jnp.where(here, m[:, lanes], moment_ref[:, cols])
    for copy in copies:
        copy.wait()


def shards(tokens, cotangent, weights, global_params, momentum, fragment):
    anywhere = pl.BlockSpec(memory_space=pl.ANY)
    vmem = pl.BlockSpec(memory_space=pltpu.VMEM)
    smem = pl.BlockSpec(memory_space=pltpu.SMEM)
    sem = pltpu.SemaphoreType.DMA
    u, g, m = pl.pallas_call(
        step_kernel,
        out_shape=(
            jax.ShapeDtypeStruct((NFRAG, DEPTH, WIDE), BF16),
            jax.ShapeDtypeStruct((SHARE, WIDE), BF16),
            jax.ShapeDtypeStruct((SHARE, WIDE), F32),
        ),
        in_specs=[anywhere, anywhere, anywhere, vmem, vmem, smem],
        out_specs=(anywhere, vmem, vmem),
        scratch_shapes=[
            pltpu.VMEM((NF * ROWS, DEPTH), BF16),
            pltpu.VMEM((NF * ROWS, DEPTH), BF16),
            pltpu.VMEM((DEPTH, NF * ROWS), BF16),
            pltpu.VMEM((DEPTH, NF * ROWS), BF16),
            pltpu.VMEM((DEPTH, 3 * HID), BF16),
            pltpu.VMEM((NFRAG, DEPTH, WIDE), BF16),
            pltpu.VMEM((NFRAG, NF, ROWS, WIDE), BF16),
            pltpu.VMEM((NFRAG, NF, ROWS, WIDE), BF16),
            pltpu.VMEM((NFRAG, NF * ROWS, WIDE), BF16),
            pltpu.VMEM((NFRAG, DEPTH, WIDE), BF16),
            pltpu.VMEM((NQ, 2, SHARE, WIDE), BF16),
            pltpu.VMEM((NQ, SHARE, WIDE), BF16),
            pltpu.VMEM((NQ, SHARE, WIDE), BF16),
            pltpu.VMEM((NQ, SHARE, WIDE), BF16),
            pltpu.VMEM((NQ, 2, SHARE, WIDE), BF16),
            sem((5,)),
            sem((2 * CHUNKS, NF - 1)),
            sem((2 * CHUNKS, NF - 1)),
            sem((2, NF - 1)),
            sem((2, NF - 1)),
            sem((2, NF - 1)),
            sem((2, NF - 1)),
            sem((2,)),
            sem((2,)),
            sem((NQ - 1,)),
            sem((NQ - 1,)),
            sem((NQ - 1,)),
            sem((NQ - 1,)),
        ],
        compiler_params=pltpu.CompilerParams(
            collective_id=0, has_side_effects=True, vmem_limit_bytes=56 * 2**20
        ),
        cost_estimate=pl.CostEstimate(
            flops=4 * ROWS * D * 3 * HID, bytes_accessed=10 * 2**20, transcendentals=ROWS * HID
        ),
    )(tokens, cotangent, weights, global_params, momentum, fragment)
    return pl.pallas_call(
        place_kernel,
        out_shape=(
            jax.ShapeDtypeStruct((1, DEPTH, 3 * HID), BF16),
            jax.ShapeDtypeStruct(global_params.shape, BF16),
            jax.ShapeDtypeStruct(momentum.shape, F32),
        ),
        in_specs=[anywhere, vmem, vmem, vmem, vmem, smem],
        out_specs=(anywhere, vmem, vmem),
        scratch_shapes=[sem((3 * NFRAG,))],
        cost_estimate=pl.CostEstimate(flops=0, bytes_accessed=6 * 2**20, transcendentals=0),
    )(u, g, m, global_params, momentum, fragment)


def solution(mesh):
    placed = (
        P(("rep", "fsdp"), None),
        P(("rep", "fsdp"), None),
        P("rep", "fsdp", None),
        P(("fsdp", "rep"), None),
        P(("fsdp", "rep"), None),
        P(),
    )
    return jax.shard_map(
        shards,
        mesh=mesh,
        in_specs=placed,
        out_specs=(P("rep", "fsdp", None), P(("fsdp", "rep"), None), P(("fsdp", "rep"), None)),
        check_vma=False,
    )
```

```python
import math

import jax
import jax.numpy as jnp
from jax import lax
from jax.experimental import pallas as pl
from jax.experimental.pallas import tpu as pltpu
from jax.sharding import PartitionSpec as P

D = 8192
FRAG = 128
NFRAG = 4
HID = 512
NF = 8
NX = 4
NZ = 8
NQ = 16
ROWS = 128
HALF = ROWS // 2
DEPTH = D // NF
SHARE = 32
WIDE = 3 * FRAG
PAIR = 2 * FRAG
CHUNKS = 4
TILE = 256
PLACE = 256


INNER_RATE = 0.5
OUTER_RATE = 0.7
MOMENT = 0.9
MIX_RATE = 0.5
SCALE_IN = 1.0 / math.sqrt(D)
SCALE_HID = 1.0 / math.sqrt(HID)
BF16 = jnp.bfloat16
F32 = jnp.float32
MESH = pl.DeviceIdType.MESH


def dot(a, b):
    return jnp.dot(a, b, preferred_element_type=F32)


def step_kernel(
    tokens,
    cotangent,
    weights,
    global_ref,
    moment_ref,
    fragment,
    u_out,
    g_out,
    m_out,
    tcut,
    ccut,
    tturn,
    cturn,
    w,
    wrot,
    ysend,
    yrecv,
    far,
    near,
    psend,
    precv,
    acts,
    u,
    u0,
    r1,
    s1,
    r2,
    gall,
    local_sem,
    a_send,
    a_recv,
    y_send,
    y_recv,
    h_send,
    h_recv,
    c_send,
    c_recv,
    s_send,
    s_recv,
    g_send,
    g_recv,
    t_send,
    t_recv,
    b_send,
    b_recv,
):
    rep = lax.axis_index("rep")
    me = lax.axis_index("fsdp")
    x, yh = me % NX, me // NX
    core, q = rep % 2, rep // 2
    z, yl = q // 2, q % 2
    frag = lax.rem(fragment[0], NFRAG)

    def fsdp_to(k):
        return (x + k % NX) % NX + NX * ((yh + k // NX) % 2)

    def fsdp_from(k):
        return (x + NX - k % NX) % NX + NX * ((yh + k // NX) % 2)

    def q_to(k):
        return ((z + k // 2) % NZ) * 2 + (yl + k % 2) % 2

    def q_from(k):
        return ((z + NZ - k // 2) % NZ) * 2 + (yl + k % 2) % 2

    def at_fsdp(f):
        return (rep, f)

    def at_q(p):
        return (p * 2 + core, me)

    partner = (q * 2 + 1 - core, me)

    def each(n, body):
        def step(k, carry):
            body(k)
            return carry

        lax.fori_loop(0, n, step, 0)

    barrier = pltpu.get_barrier_semaphore()

    def greet_fsdp(i):
        pl.semaphore_signal(barrier, inc=1, device_id=at_fsdp(fsdp_to(i + 1)), device_id_type=MESH)

    def greet_q(i):
        pl.semaphore_signal(barrier, inc=1, device_id=at_q(q_to(i + 1)), device_id_type=MESH)

    each(NF - 1, greet_fsdp)
    each(NQ - 1, greet_q)
    pl.semaphore_signal(barrier, inc=1, device_id=partner, device_id_type=MESH)

    own_cols = pl.ds(pl.multiple_of(me * DEPTH, DEPTH), DEPTH)
    own_rows = pl.ds(pl.multiple_of(me * ROWS, ROWS), ROWS)
    load_w = pltpu.make_async_copy(weights.at[0], w, local_sem.at[0])
    load_t = pltpu.make_async_copy(tokens.at[:, own_cols], tcut.at[own_rows], local_sem.at[1])
    load_c = pltpu.make_async_copy(cotangent.at[:, own_cols], ccut.at[own_rows], local_sem.at[2])
    load_w.start()
    load_t.start()
    load_c.start()
    pl.semaphore_wait(barrier, NF - 1 + NQ - 1 + 1)

    part = ROWS // CHUNKS

    def exchange(source, target, h, slot, k):
        f = fsdp_to(k)
        cols = pl.ds(pl.multiple_of(f * DEPTH, DEPTH), DEPTH)
        rows = pl.ds(pl.multiple_of(me * ROWS + h * part, part), part)
        return pltpu.make_async_remote_copy(
            src_ref=source.at[pl.ds(h * part, part), cols],
            dst_ref=target.at[rows],
            send_sem=a_send.at[slot, k - 1],
            recv_sem=a_recv.at[slot, k - 1],
            device_id=at_fsdp(f),
            device_id_type=MESH,
        )

    for h in range(CHUNKS):
        each(NF - 1, lambda i: exchange(tokens, tcut, h, h, NF - 1 - i).start())
    for h in range(CHUNKS):
        each(NF - 1, lambda i: exchange(cotangent, ccut, h, CHUNKS + h, NF - 1 - i).start())

    load_w.wait()
    for j in range(NFRAG):
        first = lax.rem(frag + j, NFRAG) * FRAG
        for member in range(3):
            cols = pl.ds(first + member * HID, FRAG)
            wrot[j, :, member * FRAG : (member + 1) * FRAG] = w[:, cols]

    def tile_of(i):
        return pl.ds(pl.multiple_of(i * TILE, TILE), TILE)

    def spread(j, i, cols, value):
        block = value.astype(BF16).reshape(TILE // ROWS, ROWS, value.shape[-1])
        ysend[j, i // 2, pl.ds(i % 2 * 2, 2), :, cols] = block

    load_t.wait()
    for h in range(CHUNKS):
        each(NF - 1, lambda i: exchange(tokens, tcut, h, h, NF - 1 - i).wait_recv())

    def forward_t(i):
        rows = tcut[tile_of(i), :]
        for j in range(NFRAG):
            spread(j, i, slice(0, PAIR), dot(rows, wrot[j, :, :PAIR]) * SCALE_IN)
        tturn[:, tile_of(i)] = rows.T

    each(NF * ROWS // TILE, forward_t)

    load_c.wait()
    for h in range(CHUNKS):
        each(NF - 1, lambda i: exchange(cotangent, ccut, h, CHUNKS + h, NF - 1 - i).wait_recv())

    def forward_c(groups):
        def run(i):
            rows = ccut[tile_of(i), :]
            for j in groups:
                spread(j, i, slice(PAIR, WIDE), dot(rows, wrot[j, :, PAIR:]) * SCALE_HID)

        return run

    def send_terms(k):
        f = fsdp_to(k)
        return pltpu.make_async_remote_copy(
            src_ref=ysend.at[0, f // NX, f % NX],
            dst_ref=yrecv.at[k],
            send_sem=y_send.at[k - 1],
            recv_sem=y_recv.at[k - 1],
            device_id=at_fsdp(f),
            device_id_type=MESH,
        )

    def block_of(j, f):
        return acts.at[j, pl.ds(pl.multiple_of(f * ROWS, ROWS), ROWS)]

    def send_acts(k):
        block = block_of(0, me)
        return pltpu.make_async_remote_copy(
            src_ref=block,
            dst_ref=block,
            send_sem=h_send.at[k - 1],
            recv_sem=h_recv.at[k - 1],
            device_id=at_fsdp(fsdp_to(k)),
            device_id_type=MESH,
        )

    def got_acts(k):
        block = block_of(0, fsdp_from(k))
        return pltpu.make_async_remote_copy(
            src_ref=block,
            dst_ref=block,
            send_sem=h_send.at[k - 1],
            recv_sem=h_recv.at[k - 1],
            device_id=at_fsdp(fsdp_to(k)),
            device_id_type=MESH,
        )

    ahead = ((x + 1) % NX, (x + 3) % NX)
    opposite = (x + 2) % NX
    beside = tuple(at_fsdp(at + NX * yh) for at in ahead)
    pole = at_fsdp(x + NX * (1 - yh))
    halves = (pl.ds(0, HALF), pl.ds(HALF, HALF))

    def hop(source, target, sends, recvs, j, slot, to):
        return pltpu.make_async_remote_copy(
            src_ref=source,
            dst_ref=target,
            send_sem=sends.at[j - 1, slot],
            recv_sem=recvs.at[j - 1, slot],
            device_id=to,
            device_id_type=MESH,
        )

    def term_far(j, way):
        return hop(
            ysend.at[j, :, opposite, halves[way]],
            far.at[j - 1, way],
            t_send,
            t_recv,
            j,
            way,
            beside[way],
        )

    def term_near(j, way, late):
        half = halves[way if late else 1 - way]
        return hop(
            ysend.at[j, :, ahead[way], half],
            near.at[j - 1, way, :, half],
            t_send,
            t_recv,
            j,
            2 + 2 * late + way,
            beside[way],
        )

    def term_pole(j):
        return hop(psend.at[j - 1], precv.at[j - 1], t_send, t_recv, j, 6, pole)

    def terms_begin(j):
        for way in range(2):
            term_far(j, way).start()
        for way in range(2):
            term_near(j, way, 0).start()

    def terms_pass(j):
        for way in range(2):
            term_far(j, way).wait_recv()
            own = ysend[j, :, ahead[way], halves[way]].astype(F32)
            sums = own + far[j - 1, way].astype(F32)
            ysend[j, :, ahead[way], halves[way]] = sums.astype(BF16)
            term_near(j, way, 1).start()

    def terms_row(j, half):
        total = ysend[j, half, x].astype(F32)
        for way in range(2):
            total = total + near[j - 1, way, half].astype(F32)
        return total

    def terms_cross(j):
        for late in range(2):
            for way in range(2):
                term_near(j, way, late).wait_recv()
        psend[j - 1] = terms_row(j, 1 - yh).astype(BF16)
        term_pole(j).start()

    def acts_begin(j):
        act_pole(j, me).start()
        for way in range(2):
            act_near(j, way, 0, x).start()

    def act_pole(j, f):
        return hop(block_of(j, f), block_of(j, f), b_send, b_recv, j, 0, pole)

    def act_near(j, way, other, at):
        block = block_of(j, at + NX * (1 - yh if other else yh))
        slot = 1 + way + 2 * other
        return hop(block, block, b_send, b_recv, j, slot, beside[way])

    def act_far(j, way, other, at):
        f = at + NX * (1 - yh if other else yh)
        rows = pl.ds(pl.multiple_of(f * ROWS + way * HALF, HALF), HALF)
        block = acts.at[j, rows]
        slot = 5 + way + 2 * other
        return hop(block, block, b_send, b_recv, j, slot, beside[way])

    def acts_turn(j):
        act_pole(j, x + NX * (1 - yh)).wait_recv()
        for way in range(2):
            act_near(j, way, 1, x).start()

    def acts_pass(j, other):
        for way in range(2):
            act_near(j, way, other, ahead[1 - way]).wait_recv()
            act_far(j, way, other, ahead[1 - way]).start()

    def acts_end(j):
        for other in range(2):
            for way in range(2):
                act_far(j, way, other, opposite).wait_recv()

    def rest_left(j):
        for way in range(2):
            term_far(j, way).wait_send()
            term_near(j, way, 0).wait_send()
            term_near(j, way, 1).wait_send()
            for other in range(2):
                act_near(j, way, other, x).wait_send()
                act_far(j, way, other, opposite).wait_send()
        term_pole(j).wait_send()
        act_pole(j, me).wait_send()

    rest = (1, 2, 3)
    tiles = NF * ROWS // TILE
    each(tiles, forward_c((0,)))
    each(NF - 1, lambda i: send_terms(i + 1).start())
    for j in rest:
        each(tiles, forward_c((j,)))
        terms_begin(j)

    def turn_c(i):
        cturn[:, tile_of(i)] = ccut[tile_of(i), :].T

    each(tiles, turn_c)

    def activate(j, total):
        gate = total[:, :FRAG]
        up = total[:, FRAG:PAIR]
        hidden_grad = total[:, PAIR:]
        sigmoid = jax.nn.sigmoid(gate)
        silu = gate * sigmoid
        acts[j, own_rows, :FRAG] = (
            hidden_grad * up * sigmoid * (1.0 + gate * (1.0 - sigmoid))
        ).astype(BF16)
        acts[j, own_rows, FRAG:PAIR] = (hidden_grad * silu).astype(BF16)
        acts[j, own_rows, PAIR:] = (silu * up).astype(BF16)

    def descend(j, i):
        rows = tile_of(i)
        grad_in = dot(tturn[rows, :], acts[j, :, :PAIR]) * SCALE_IN
        grad_down = dot(cturn[rows, :], acts[j, :, PAIR:]) * SCALE_HID
        left = wrot[j, rows, :PAIR].astype(F32) - INNER_RATE * grad_in
        right = wrot[j, rows, PAIR:].astype(F32) - INNER_RATE * grad_down
        return left.astype(BF16), right.astype(BF16)

    each(NF - 1, lambda i: send_terms(i + 1).wait_recv())
    total = ysend[0, yh, x].astype(F32)
    for k in range(1, NF):
        total = total + yrecv[k].astype(F32)
    activate(0, total)
    each(NF - 1, lambda i: send_acts(i + 1).start())
    for j in rest:
        terms_pass(j)
    each(NF - 1, lambda i: got_acts(i + 1).wait_recv())

    span = TILE // (2 * SHARE)

    def descend_first(i):
        left, right = descend(0, i)
        at = pl.ds(i * span, span)
        u0[at, :, :, :PAIR] = left.reshape(span, 2, SHARE, PAIR)
        u0[at, :, :, PAIR:] = right.reshape(span, 2, SHARE, FRAG)

    each(DEPTH // TILE, descend_first)

    across = pltpu.make_async_remote_copy(
        src_ref=u0.at[:, 1 - core],
        dst_ref=r1,
        send_sem=c_send.at[0],
        recv_sem=c_recv.at[0],
        device_id=partner,
        device_id_type=MESH,
    )
    across.start()

    for j in rest:
        terms_cross(j)

    across.wait()
    s1[...] = (u0[:, core].astype(F32) + r1[...].astype(F32)).astype(BF16)

    def send_sum(k):
        p = q_to(k)
        return pltpu.make_async_remote_copy(
            src_ref=s1.at[p],
            dst_ref=r2.at[k],
            send_sem=s_send.at[k - 1],
            recv_sem=s_recv.at[k - 1],
            device_id=at_q(p),
            device_id_type=MESH,
        )

    each(NQ - 1, lambda i: send_sum(i + 1).start())
    for j in rest:
        term_pole(j).wait_recv()
        activate(j, terms_row(j, yh) + precv[j - 1].astype(F32))
        acts_begin(j)
    each(NQ - 1, lambda i: send_sum(i + 1).wait_recv())

    total = s1[q].astype(F32)
    for k in range(1, NQ):
        total = total + r2[k].astype(F32)
    first = frag * FRAG
    for member in range(3):
        cols = pl.ds(first + member * HID, FRAG)
        lanes = slice(member * FRAG, (member + 1) * FRAG)
        old = global_ref[:, cols].astype(F32)
        average = old - total[:, lanes] / (2 * NQ)
        moment = MOMENT * moment_ref[:, cols] + average
        m_out[:, lanes] = moment
        gall[q, core, :, lanes] = (old - OUTER_RATE * (average + MOMENT * moment)).astype(BF16)
    g_out[...] = gall[q, core]

    def send_global(k):
        block = gall.at[q, core]
        return pltpu.make_async_remote_copy(
            src_ref=block,
            dst_ref=block,
            send_sem=g_send.at[k - 1],
            recv_sem=g_recv.at[k - 1],
            device_id=at_q(q_to(k)),
            device_id_type=MESH,
        )

    def got_global(k):
        block = gall.at[q_from(k), core]
        return pltpu.make_async_remote_copy(
            src_ref=block,
            dst_ref=block,
            send_sem=g_send.at[k - 1],
            recv_sem=g_recv.at[k - 1],
            device_id=at_q(q_to(k)),
            device_id_type=MESH,
        )

    each(NQ - 1, lambda i: send_global(i + 1).start())

    for j in rest:
        acts_turn(j)
        acts_pass(j, 0)
    for j in rest:
        acts_pass(j, 1)
    for j in rest:
        acts_end(j)

    def descend_rest(i):
        for j in range(1, NFRAG):
            left, right = descend(j, i)
            u[j, tile_of(i), :PAIR] = left
            u[j, tile_of(i), PAIR:] = right

    each(DEPTH // TILE, descend_rest)
    store_rest = pltpu.make_async_copy(
        u.at[pl.ds(1, 3)], u_out.at[pl.ds(1, 3)], local_sem.at[3]
    )
    store_rest.start()

    each(NQ - 1, lambda i: got_global(i + 1).wait_recv())
    side = gall.at[:, core]
    give = pltpu.make_async_remote_copy(
        src_ref=side,
        dst_ref=side,
        send_sem=c_send.at[1],
        recv_sem=c_recv.at[1],
        device_id=partner,
        device_id_type=MESH,
    )
    give.start()

    for h in range(CHUNKS):
        each(NF - 1, lambda i: exchange(tokens, tcut, h, h, NF - 1 - i).wait_send())
        each(NF - 1, lambda i: exchange(cotangent, ccut, h, CHUNKS + h, NF - 1 - i).wait_send())
    each(NF - 1, lambda i: send_terms(i + 1).wait_send())
    each(NF - 1, lambda i: send_acts(i + 1).wait_send())
    for j in rest:
        rest_left(j)
    each(NQ - 1, lambda i: send_sum(i + 1).wait_send())
    each(NQ - 1, lambda i: send_global(i + 1).wait_send())

    give.wait_send()
    other = gall.at[:, 1 - core]
    pltpu.make_async_remote_copy(
        src_ref=other,
        dst_ref=other,
        send_sem=c_send.at[1],
        recv_sem=c_recv.at[1],
        device_id=partner,
        device_id_type=MESH,
    ).wait_recv()

    def mix(i):
        at = pl.ds(i * span, span)
        mixed = MIX_RATE * u0[at].astype(F32) + (1.0 - MIX_RATE) * gall[at].astype(F32)
        u[0, tile_of(i), :] = mixed.astype(BF16).reshape(TILE, WIDE)

    each(DEPTH // TILE, mix)
    store_first = pltpu.make_async_copy(u.at[0], u_out.at[0], local_sem.at[4])
    store_first.start()
    store_first.wait()
    store_rest.wait()


def place_kernel(u, g, m, global_ref, moment_ref, fragment, w_out, g_out, m_out):
    frag = lax.rem(fragment[0], NFRAG)
    for at in range(NFRAG):
        j = lax.rem(at + NFRAG - frag, NFRAG)
        for member in range(3):
            cols = slice(member * HID + at * FRAG, member * HID + (at + 1) * FRAG)
            w_out[0, :, cols] = u[j, :, member * FRAG : (member + 1) * FRAG]

    @pl.when(pl.program_id(0) == 0)
    def _():
        for at in range(NFRAG):
            here = frag == at
            for member in range(3):
                cols = slice(member * HID + at * FRAG, member * HID + (at + 1) * FRAG)
                lanes = slice(member * FRAG, (member + 1) * FRAG)
                g_out[:, cols] = jnp.where(here, g[:, lanes], global_ref[:, cols])
                m_out[:, cols] = jnp.where(here, m[:, lanes], moment_ref[:, cols])


def shards(tokens, cotangent, weights, global_params, momentum, fragment):
    anywhere = pl.BlockSpec(memory_space=pl.ANY)
    vmem = pl.BlockSpec(memory_space=pltpu.VMEM)
    smem = pl.BlockSpec(memory_space=pltpu.SMEM)
    sem = pltpu.SemaphoreType.DMA
    u, g, m = pl.pallas_call(
        step_kernel,
        out_shape=(
            jax.ShapeDtypeStruct((NFRAG, DEPTH, WIDE), BF16),
            jax.ShapeDtypeStruct((SHARE, WIDE), BF16),
            jax.ShapeDtypeStruct((SHARE, WIDE), F32),
        ),
        in_specs=[anywhere, anywhere, anywhere, vmem, vmem, smem],
        out_specs=(anywhere, vmem, vmem),
        scratch_shapes=[
            pltpu.VMEM((NF * ROWS, DEPTH), BF16),
            pltpu.VMEM((NF * ROWS, DEPTH), BF16),
            pltpu.VMEM((DEPTH, NF * ROWS), BF16),
            pltpu.VMEM((DEPTH, NF * ROWS), BF16),
            pltpu.VMEM((DEPTH, 3 * HID), BF16),
            pltpu.VMEM((NFRAG, DEPTH, WIDE), BF16),
            pltpu.VMEM((NFRAG, 2, NX, ROWS, WIDE), BF16),
            pltpu.VMEM((NF, ROWS, WIDE), BF16),
            pltpu.VMEM((NFRAG - 1, 2, 2, HALF, WIDE), BF16),
            pltpu.VMEM((NFRAG - 1, 2, 2, ROWS, WIDE), BF16),
            pltpu.VMEM((NFRAG - 1, ROWS, WIDE), BF16),
            pltpu.VMEM((NFRAG - 1, ROWS, WIDE), BF16),
            pltpu.VMEM((NFRAG, NF * ROWS, WIDE), BF16),
            pltpu.VMEM((NFRAG, DEPTH, WIDE), BF16),
            pltpu.VMEM((NQ, 2, SHARE, WIDE), BF16),
            pltpu.VMEM((NQ, SHARE, WIDE), BF16),
            pltpu.VMEM((NQ, SHARE, WIDE), BF16),
            pltpu.VMEM((NQ, SHARE, WIDE), BF16),
            pltpu.VMEM((NQ, 2, SHARE, WIDE), BF16),
            sem((5,)),
            sem((2 * CHUNKS, NF - 1)),
            sem((2 * CHUNKS, NF - 1)),
            sem((NF - 1,)),
            sem((NF - 1,)),
            sem((NF - 1,)),
            sem((NF - 1,)),
            sem((2,)),
            sem((2,)),
            sem((NQ - 1,)),
            sem((NQ - 1,)),
            sem((NQ - 1,)),
            sem((NQ - 1,)),
            sem((NFRAG - 1, 7)),
            sem((NFRAG - 1, 7)),
            sem((NFRAG - 1, 9)),
            sem((NFRAG - 1, 9)),
        ],
        compiler_params=pltpu.CompilerParams(
            collective_id=0, has_side_effects=True, vmem_limit_bytes=56 * 2**20
        ),
        cost_estimate=pl.CostEstimate(
            flops=4 * ROWS * D * 3 * HID, bytes_accessed=10 * 2**20, transcendentals=ROWS * HID
        ),
    )(tokens, cotangent, weights, global_params, momentum, fragment)
    return pl.pallas_call(
        place_kernel,
        out_shape=(
            jax.ShapeDtypeStruct((1, DEPTH, 3 * HID), BF16),
            jax.ShapeDtypeStruct(global_params.shape, BF16),
            jax.ShapeDtypeStruct(momentum.shape, F32),
        ),
        grid=(DEPTH // PLACE,),
        in_specs=[
            pl.BlockSpec((NFRAG, PLACE, WIDE), lambda i: (0, i, 0)),
            vmem,
            vmem,
            vmem,
            vmem,
            smem,
        ],
        out_specs=(pl.BlockSpec((1, PLACE, 3 * HID), lambda i: (0, i, 0)), vmem, vmem),
        cost_estimate=pl.CostEstimate(flops=0, bytes_accessed=6 * 2**20, transcendentals=0),
    )(u, g, m, global_params, momentum, fragment)


def solution(mesh):
    placed = (
        P(("rep", "fsdp"), None),
        P(("rep", "fsdp"), None),
        P("rep", "fsdp", None),
        P(("fsdp", "rep"), None),
        P(("fsdp", "rep"), None),
        P(),
    )
    return jax.shard_map(
        shards,
        mesh=mesh,
        in_specs=placed,
        out_specs=(P("rep", "fsdp", None), P(("fsdp", "rep"), None), P(("fsdp", "rep"), None)),
        check_vma=False,
    )
```

```python
import math

import jax
import jax.numpy as jnp
from jax import lax
from jax.experimental import pallas as pl
from jax.experimental.pallas import tpu as pltpu
from jax.sharding import PartitionSpec as P

D = 8192
FRAG = 128
NFRAG = 4
HID = 512
NF = 8
NX = 4
NZ = 8
NQ = 16
ROWS = 128
HALF = ROWS // 2
DEPTH = D // NF
SHARE = 32
WIDE = 3 * FRAG
PAIR = 2 * FRAG
CHUNKS = 4
TILE = 256
PLACE = 256


INNER_RATE = 0.5
OUTER_RATE = 0.7
MOMENT = 0.9
MIX_RATE = 0.5
SCALE_IN = 1.0 / math.sqrt(D)
SCALE_HID = 1.0 / math.sqrt(HID)
BF16 = jnp.bfloat16
F32 = jnp.float32
MESH = pl.DeviceIdType.MESH


def dot(a, b):
    return jnp.dot(a, b, preferred_element_type=F32)


def step_kernel(
    tokens,
    cotangent,
    weights,
    global_ref,
    moment_ref,
    fragment,
    u_out,
    g_out,
    m_out,
    tcut,
    ccut,
    tturn,
    cturn,
    w,
    wrot,
    ysend,
    yrecv,
    far,
    near,
    psend,
    precv,
    prow,
    acts,
    u,
    u0,
    r1,
    s1,
    r2,
    gall,
    local_sem,
    a_send,
    a_recv,
    y_send,
    y_recv,
    h_send,
    h_recv,
    c_send,
    c_recv,
    s_send,
    s_recv,
    g_send,
    g_recv,
    t_send,
    t_recv,
    b_send,
    b_recv,
):
    rep = lax.axis_index("rep")
    me = lax.axis_index("fsdp")
    x, yh = me % NX, me // NX
    core, q = rep % 2, rep // 2
    z, yl = q // 2, q % 2
    frag = lax.rem(fragment[0], NFRAG)

    def fsdp_to(k):
        return (x + k % NX) % NX + NX * ((yh + k // NX) % 2)

    def fsdp_from(k):
        return (x + NX - k % NX) % NX + NX * ((yh + k // NX) % 2)

    def q_to(k):
        return ((z + k // 2) % NZ) * 2 + (yl + k % 2) % 2

    def q_from(k):
        return ((z + NZ - k // 2) % NZ) * 2 + (yl + k % 2) % 2

    def at_fsdp(f):
        return (rep, f)

    def at_q(p):
        return (p * 2 + core, me)

    partner = (q * 2 + 1 - core, me)

    def each(n, body):
        def step(k, carry):
            body(k)
            return carry

        lax.fori_loop(0, n, step, 0)

    barrier = pltpu.get_barrier_semaphore()

    def greet_fsdp(i):
        pl.semaphore_signal(barrier, inc=1, device_id=at_fsdp(fsdp_to(i + 1)), device_id_type=MESH)

    def greet_q(i):
        pl.semaphore_signal(barrier, inc=1, device_id=at_q(q_to(i + 1)), device_id_type=MESH)

    each(NF - 1, greet_fsdp)
    each(NQ - 1, greet_q)
    pl.semaphore_signal(barrier, inc=1, device_id=partner, device_id_type=MESH)

    own_cols = pl.ds(pl.multiple_of(me * DEPTH, DEPTH), DEPTH)
    own_rows = pl.ds(pl.multiple_of(me * ROWS, ROWS), ROWS)
    load_w = pltpu.make_async_copy(weights.at[0], w, local_sem.at[0])
    load_t = pltpu.make_async_copy(tokens.at[:, own_cols], tcut.at[own_rows], local_sem.at[1])
    load_c = pltpu.make_async_copy(cotangent.at[:, own_cols], ccut.at[own_rows], local_sem.at[2])
    load_w.start()
    load_t.start()
    load_c.start()
    pl.semaphore_wait(barrier, NF - 1 + NQ - 1 + 1)

    def all_of(block, send, recv):
        return pltpu.make_async_remote_copy(
            src_ref=block,
            dst_ref=block,
            send_sem=send,
            recv_sem=recv,
            device_id=partner,
            device_id_type=MESH,
        )

    others = pl.ds(0, (NF - 1) * ROWS)

    part = ROWS // CHUNKS

    def exchange(source, target, h, slot, k):
        f = fsdp_to(k)
        cols = pl.ds(pl.multiple_of(f * DEPTH, DEPTH), DEPTH)
        rows = pl.ds(pl.multiple_of(me * ROWS + h * part, part), part)
        return pltpu.make_async_remote_copy(
            src_ref=source.at[pl.ds(h * part, part), cols],
            dst_ref=target.at[rows],
            send_sem=a_send.at[slot],
            recv_sem=a_recv.at[slot],
            device_id=at_fsdp(f),
            device_id_type=MESH,
        )

    for h in range(CHUNKS):
        each(NF - 1, lambda i: exchange(tokens, tcut, h, 0, NF - 1 - i).start())
    for h in range(CHUNKS):
        each(NF - 1, lambda i: exchange(cotangent, ccut, h, 1, NF - 1 - i).start())

    load_w.wait()
    for j in range(NFRAG):
        first = lax.rem(frag + j, NFRAG) * FRAG
        for member in range(3):
            cols = pl.ds(first + member * HID, FRAG)
            wrot[j, :, member * FRAG : (member + 1) * FRAG] = w[:, cols]

    def tile_of(i):
        return pl.ds(pl.multiple_of(i * TILE, TILE), TILE)

    def spread(j, i, cols, value):
        block = value.astype(BF16).reshape(TILE // ROWS, ROWS, value.shape[-1])
        ysend[j, i // 2, pl.ds(i % 2 * 2, 2), :, cols] = block

    load_t.wait()
    all_of(tcut.at[others], a_send.at[0], a_recv.at[0]).wait_recv()

    def forward_t(i):
        rows = tcut[tile_of(i), :]
        for j in range(NFRAG):
            spread(j, i, slice(0, PAIR), dot(rows, wrot[j, :, :PAIR]) * SCALE_IN)
        tturn[:, tile_of(i)] = rows.T

    each(NF * ROWS // TILE, forward_t)

    load_c.wait()
    all_of(ccut.at[others], a_send.at[1], a_recv.at[1]).wait_recv()

    def forward_c(groups):
        def run(i):
            rows = ccut[tile_of(i), :]
            for j in groups:
                spread(j, i, slice(PAIR, WIDE), dot(rows, wrot[j, :, PAIR:]) * SCALE_HID)

        return run

    def send_terms(k):
        f = fsdp_to(k)
        return pltpu.make_async_remote_copy(
            src_ref=ysend.at[0, f // NX, f % NX],
            dst_ref=yrecv.at[k],
            send_sem=y_send.at[0],
            recv_sem=y_recv.at[0],
            device_id=at_fsdp(f),
            device_id_type=MESH,
        )

    def block_of(j, f):
        return acts.at[j, pl.ds(pl.multiple_of(f * ROWS, ROWS), ROWS)]

    def send_acts(k):
        block = block_of(0, me)
        return pltpu.make_async_remote_copy(
            src_ref=block,
            dst_ref=block,
            send_sem=h_send.at[0],
            recv_sem=h_recv.at[0],
            device_id=at_fsdp(fsdp_to(k)),
            device_id_type=MESH,
        )

    sent_terms = all_of(yrecv.at[pl.ds(1, NF - 1)], y_send.at[0], y_recv.at[0])
    sent_acts = all_of(acts.at[0, others], h_send.at[0], h_recv.at[0])

    ahead = ((x + 1) % NX, (x + 3) % NX)
    opposite = (x + 2) % NX
    beside = tuple(at_fsdp(at + NX * yh) for at in ahead)
    pole = at_fsdp(x + NX * (1 - yh))
    halves = (pl.ds(0, HALF), pl.ds(HALF, HALF))
    first_row = (1, 2)
    first_pole = (3,)

    def hop(source, target, sends, recvs, j, slot, to):
        return pltpu.make_async_remote_copy(
            src_ref=source,
            dst_ref=target,
            send_sem=sends.at[0],
            recv_sem=recvs.at[j - 1, slot],
            device_id=to,
            device_id_type=MESH,
        )

    def span_of(j):
        return pl.ds(yh, 1) if j in first_pole else pl.ds(0, 2)

    def seat_of(j):
        return pl.ds(0, 1) if j in first_pole else pl.ds(0, 2)

    def term_far(j, way):
        return hop(
            ysend.at[j, span_of(j), opposite, halves[way]],
            far.at[j - 1, way, seat_of(j)],
            t_send,
            t_recv,
            j,
            way,
            beside[way],
        )

    def term_near(j, way, late):
        half = halves[way if late else 1 - way]
        return hop(
            ysend.at[j, span_of(j), ahead[way], half],
            near.at[j - 1, way, seat_of(j), half],
            t_send,
            t_recv,
            j,
            2,
            beside[way],
        )

    def term_pole(j):
        if j in first_pole:
            return hop(ysend.at[j, 1 - yh], prow, t_send, t_recv, j, 3, pole)
        return hop(psend.at[j - 1], precv.at[j - 1], t_send, t_recv, j, 3, pole)

    def terms_far(j):
        for way in range(2):
            term_far(j, way).start()

    def terms_near(j):
        for way in range(2):
            term_near(j, way, 0).start()

    def terms_row_in(j):
        term_pole(j).wait_recv()
        ysend[j, yh] = (ysend[j, yh].astype(F32) + prow[...].astype(F32)).astype(BF16)

    def terms_pass(j):
        for way in range(2):
            term_far(j, way).wait_recv()
            own = ysend[j, span_of(j), ahead[way], halves[way]].astype(F32)
            sums = own + far[j - 1, way, seat_of(j)].astype(F32)
            ysend[j, span_of(j), ahead[way], halves[way]] = sums.astype(BF16)
            term_near(j, way, 1).start()

    def terms_got(j):
        all_of(near.at[j - 1, :, seat_of(j)], t_send.at[0], t_recv.at[j - 1, 2]).wait_recv()

    def terms_row(j, half, seat):
        total = ysend[j, half, x].astype(F32)
        for way in range(2):
            total = total + near[j - 1, way, seat].astype(F32)
        return total

    def terms_cross(j):
        terms_got(j)
        psend[j - 1] = terms_row(j, 1 - yh, 1 - yh).astype(BF16)
        term_pole(j).start()

    def terms_end(j):
        if j in first_pole:
            terms_got(j)
            activate(j, terms_row(j, yh, 0))
        else:
            term_pole(j).wait_recv()
            activate(j, terms_row(j, yh, yh) + precv[j - 1].astype(F32))

    def act_pole(j, f):
        return hop(block_of(j, f), block_of(j, f), b_send, b_recv, j, 0, pole)

    def act_near(j, way, other, at):
        block = block_of(j, at + NX * (1 - yh if other else yh))
        slot = 1 + way + 2 * other
        return hop(block, block, b_send, b_recv, j, slot, beside[way])

    def act_far(j, way, other, at):
        f = at + NX * (1 - yh if other else yh)
        rows = pl.ds(pl.multiple_of(f * ROWS + way * HALF, HALF), HALF)
        block = acts.at[j, rows]
        return hop(block, block, b_send, b_recv, j, 5, beside[way])

    def acts_begin(j):
        act_pole(j, me).start()
        for way in range(2):
            act_near(j, way, 0, x).start()

    def acts_turn(j):
        act_pole(j, x + NX * (1 - yh)).wait_recv()
        for way in range(2):
            act_near(j, way, 1, x).start()

    def acts_pass(j, other):
        for way in range(2):
            act_near(j, way, other, ahead[1 - way]).wait_recv()
            act_far(j, way, other, ahead[1 - way]).start()

    def acts_all(j, blocks, slot):
        return all_of(acts.at[j, pl.ds(0, blocks * ROWS)], b_send.at[0], b_recv.at[j - 1, slot])

    def acts_across(j):
        for way in range(2):
            act_near(j, way, 0, ahead[1 - way]).wait_recv()
            act_far(j, way, 0, ahead[1 - way]).start()
            act_pole(j, ahead[1 - way] + NX * yh).start()

    def acts_last(j):
        acts_all(j, 1, 5).wait_recv()
        act_pole(j, opposite + NX * yh).start()

    def acts_end(j):
        if j in first_pole:
            acts_all(j, NX, 0).wait_recv()
        else:
            acts_all(j, 2, 5).wait_recv()

    tiles = NF * ROWS // TILE
    each(tiles, forward_c((0,)))
    each(NF - 1, lambda i: send_terms(i + 1).start())
    for j in first_pole:
        each(tiles, forward_c((j,)))
        term_pole(j).start()
    for j in first_row:
        each(tiles, forward_c((j,)))
        terms_far(j)

    def turn_c(i):
        cturn[:, tile_of(i)] = ccut[tile_of(i), :].T

    each(tiles, turn_c)

    def activate(j, total):
        gate = total[:, :FRAG]
        up = total[:, FRAG:PAIR]
        hidden_grad = total[:, PAIR:]
        sigmoid = jax.nn.sigmoid(gate)
        silu = gate * sigmoid
        acts[j, own_rows, :FRAG] = (
            hidden_grad * up * sigmoid * (1.0 + gate * (1.0 - sigmoid))
        ).astype(BF16)
        acts[j, own_rows, FRAG:PAIR] = (hidden_grad * silu).astype(BF16)
        acts[j, own_rows, PAIR:] = (silu * up).astype(BF16)

    def descend(j, i):
        rows = tile_of(i)
        grad_in = dot(tturn[rows, :], acts[j, :, :PAIR]) * SCALE_IN
        grad_down = dot(cturn[rows, :], acts[j, :, PAIR:]) * SCALE_HID
        left = wrot[j, rows, :PAIR].astype(F32) - INNER_RATE * grad_in
        right = wrot[j, rows, PAIR:].astype(F32) - INNER_RATE * grad_down
        return left.astype(BF16), right.astype(BF16)

    sent_terms.wait_recv()
    total = ysend[0, yh, x].astype(F32)
    for k in range(1, NF):
        total = total + yrecv[k].astype(F32)
    activate(0, total)
    each(NF - 1, lambda i: send_acts(i + 1).start())
    for j in first_row:
        terms_near(j)
    for j in first_row:
        terms_pass(j)
    for j in first_pole:
        terms_row_in(j)
        terms_far(j)
        terms_near(j)
    sent_acts.wait_recv()

    span = TILE // (2 * SHARE)

    def descend_first(i):
        left, right = descend(0, i)
        at = pl.ds(i * span, span)
        u0[at, :, :, :PAIR] = left.reshape(span, 2, SHARE, PAIR)
        u0[at, :, :, PAIR:] = right.reshape(span, 2, SHARE, FRAG)

    each(DEPTH // TILE, descend_first)

    across = pltpu.make_async_remote_copy(
        src_ref=u0.at[:, 1 - core],
        dst_ref=r1,
        send_sem=c_send.at[0],
        recv_sem=c_recv.at[0],
        device_id=partner,
        device_id_type=MESH,
    )
    across.start()

    for j in first_row:
        terms_cross(j)
    for j in first_pole:
        terms_pass(j)

    across.wait()
    s1[...] = (u0[:, core].astype(F32) + r1[...].astype(F32)).astype(BF16)

    def send_sum(k):
        p = q_to(k)
        return pltpu.make_async_remote_copy(
            src_ref=s1.at[p],
            dst_ref=r2.at[k],
            send_sem=s_send.at[0],
            recv_sem=s_recv.at[0],
            device_id=at_q(p),
            device_id_type=MESH,
        )

    each(NQ - 1, lambda i: send_sum(i + 1).start())
    for j in first_row + first_pole:
        terms_end(j)
        acts_begin(j)
    sent_sums = all_of(r2.at[pl.ds(1, NQ - 1)], s_send.at[0], s_recv.at[0])
    sent_sums.wait_recv()

    total = s1[q].astype(F32)
    for k in range(1, NQ):
        total = total + r2[k].astype(F32)
    first = frag * FRAG
    for member in range(3):
        cols = pl.ds(first + member * HID, FRAG)
        lanes = slice(member * FRAG, (member + 1) * FRAG)
        old = global_ref[:, cols].astype(F32)
        average = old - total[:, lanes] / (2 * NQ)
        moment = MOMENT * moment_ref[:, cols] + average
        m_out[:, lanes] = moment
        gall[q, core, :, lanes] = (old - OUTER_RATE * (average + MOMENT * moment)).astype(BF16)
    g_out[...] = gall[q, core]

    def send_global(k):
        block = gall.at[q, core]
        return pltpu.make_async_remote_copy(
            src_ref=block,
            dst_ref=block,
            send_sem=g_send.at[0],
            recv_sem=g_recv.at[0],
            device_id=at_q(q_to(k)),
            device_id_type=MESH,
        )

    sent_global = all_of(gall.at[pl.ds(0, NQ - 1), core], g_send.at[0], g_recv.at[0])
    each(NQ - 1, lambda i: send_global(i + 1).start())

    for j in first_row:
        acts_turn(j)
    for j in first_pole:
        acts_across(j)
    for j in first_row:
        acts_pass(j, 0)
    for j in first_pole:
        acts_last(j)
    for j in first_row:
        acts_pass(j, 1)

    def descend_rest(j):
        def run(i):
            left, right = descend(j, i)
            u[j, tile_of(i), :PAIR] = left
            u[j, tile_of(i), PAIR:] = right

        return run

    def store(j):
        return pltpu.make_async_copy(u.at[j], u_out.at[j], local_sem.at[3 + j])

    for j in first_row + first_pole:
        acts_end(j)
        each(DEPTH // TILE, descend_rest(j))
        store(j).start()

    sent_global.wait_recv()
    side = gall.at[:, core]
    give = pltpu.make_async_remote_copy(
        src_ref=side,
        dst_ref=side,
        send_sem=c_send.at[1],
        recv_sem=c_recv.at[1],
        device_id=partner,
        device_id_type=MESH,
    )
    give.start()

    all_of(tcut.at[others], a_send.at[0], a_recv.at[0]).wait_send()
    all_of(ccut.at[others], a_send.at[1], a_recv.at[1]).wait_send()
    sent_terms.wait_send()
    sent_acts.wait_send()
    every = acts.at[pl.ds(0, NFRAG - 1), others]
    all_of(every, t_send.at[0], t_recv.at[0, 0]).wait_send()
    all_of(every, b_send.at[0], b_recv.at[0, 0]).wait_send()
    sent_sums.wait_send()
    sent_global.wait_send()

    give.wait_send()
    other = gall.at[:, 1 - core]
    pltpu.make_async_remote_copy(
        src_ref=other,
        dst_ref=other,
        send_sem=c_send.at[1],
        recv_sem=c_recv.at[1],
        device_id=partner,
        device_id_type=MESH,
    ).wait_recv()

    def mix(i):
        at = pl.ds(i * span, span)
        mixed = MIX_RATE * u0[at].astype(F32) + (1.0 - MIX_RATE) * gall[at].astype(F32)
        u[0, tile_of(i), :] = mixed.astype(BF16).reshape(TILE, WIDE)

    each(DEPTH // TILE, mix)
    store(0).start()
    for j in range(NFRAG):
        store(j).wait()


def place_kernel(u, g, m, global_ref, moment_ref, fragment, w_out, g_out, m_out):
    frag = lax.rem(fragment[0], NFRAG)
    for at in range(NFRAG):
        j = lax.rem(at + NFRAG - frag, NFRAG)
        for member in range(3):
            cols = slice(member * HID + at * FRAG, member * HID + (at + 1) * FRAG)
            w_out[0, :, cols] = u[j, :, member * FRAG : (member + 1) * FRAG]

    @pl.when(pl.program_id(0) == 0)
    def _():
        for at in range(NFRAG):
            here = frag == at
            for member in range(3):
                cols = slice(member * HID + at * FRAG, member * HID + (at + 1) * FRAG)
                lanes = slice(member * FRAG, (member + 1) * FRAG)
                g_out[:, cols] = jnp.where(here, g[:, lanes], global_ref[:, cols])
                m_out[:, cols] = jnp.where(here, m[:, lanes], moment_ref[:, cols])


def shards(tokens, cotangent, weights, global_params, momentum, fragment):
    anywhere = pl.BlockSpec(memory_space=pl.ANY)
    vmem = pl.BlockSpec(memory_space=pltpu.VMEM)
    smem = pl.BlockSpec(memory_space=pltpu.SMEM)
    sem = pltpu.SemaphoreType.DMA
    u, g, m = pl.pallas_call(
        step_kernel,
        out_shape=(
            jax.ShapeDtypeStruct((NFRAG, DEPTH, WIDE), BF16),
            jax.ShapeDtypeStruct((SHARE, WIDE), BF16),
            jax.ShapeDtypeStruct((SHARE, WIDE), F32),
        ),
        in_specs=[anywhere, anywhere, anywhere, vmem, vmem, smem],
        out_specs=(anywhere, vmem, vmem),
        scratch_shapes=[
            pltpu.VMEM((NF * ROWS, DEPTH), BF16),
            pltpu.VMEM((NF * ROWS, DEPTH), BF16),
            pltpu.VMEM((DEPTH, NF * ROWS), BF16),
            pltpu.VMEM((DEPTH, NF * ROWS), BF16),
            pltpu.VMEM((DEPTH, 3 * HID), BF16),
            pltpu.VMEM((NFRAG, DEPTH, WIDE), BF16),
            pltpu.VMEM((NFRAG, 2, NX, ROWS, WIDE), BF16),
            pltpu.VMEM((NF, ROWS, WIDE), BF16),
            pltpu.VMEM((NFRAG - 1, 2, 2, HALF, WIDE), BF16),
            pltpu.VMEM((NFRAG - 1, 2, 2, ROWS, WIDE), BF16),
            pltpu.VMEM((NFRAG - 1, ROWS, WIDE), BF16),
            pltpu.VMEM((NFRAG - 1, ROWS, WIDE), BF16),
            pltpu.VMEM((NX, ROWS, WIDE), BF16),
            pltpu.VMEM((NFRAG, NF * ROWS, WIDE), BF16),
            pltpu.VMEM((NFRAG, DEPTH, WIDE), BF16),
            pltpu.VMEM((NQ, 2, SHARE, WIDE), BF16),
            pltpu.VMEM((NQ, SHARE, WIDE), BF16),
            pltpu.VMEM((NQ, SHARE, WIDE), BF16),
            pltpu.VMEM((NQ, SHARE, WIDE), BF16),
            pltpu.VMEM((NQ, 2, SHARE, WIDE), BF16),
            sem((3 + NFRAG,)),
            sem((2,)),
            sem((2,)),
            sem((1,)),
            sem((1,)),
            sem((1,)),
            sem((1,)),
            sem((2,)),
            sem((2,)),
            sem((1,)),
            sem((1,)),
            sem((1,)),
            sem((1,)),
            sem((1,)),
            sem((NFRAG - 1, 4)),
            sem((1,)),
            sem((NFRAG - 1, 6)),
        ],
        compiler_params=pltpu.CompilerParams(
            collective_id=0, has_side_effects=True, vmem_limit_bytes=56 * 2**20
        ),
        cost_estimate=pl.CostEstimate(
            flops=4 * ROWS * D * 3 * HID, bytes_accessed=10 * 2**20, transcendentals=ROWS * HID
        ),
    )(tokens, cotangent, weights, global_params, momentum, fragment)
    return pl.pallas_call(
        place_kernel,
        out_shape=(
            jax.ShapeDtypeStruct((1, DEPTH, 3 * HID), BF16),
            jax.ShapeDtypeStruct(global_params.shape, BF16),
            jax.ShapeDtypeStruct(momentum.shape, F32),
        ),
        grid=(DEPTH // PLACE,),
        in_specs=[
            pl.BlockSpec((NFRAG, PLACE, WIDE), lambda i: (0, i, 0)),
            vmem,
            vmem,
            vmem,
            vmem,
            smem,
        ],
        out_specs=(pl.BlockSpec((1, PLACE, 3 * HID), lambda i: (0, i, 0)), vmem, vmem),
        cost_estimate=pl.CostEstimate(flops=0, bytes_accessed=6 * 2**20, transcendentals=0),
    )(u, g, m, global_params, momentum, fragment)


def solution(mesh):
    placed = (
        P(("rep", "fsdp"), None),
        P(("rep", "fsdp"), None),
        P("rep", "fsdp", None),
        P(("fsdp", "rep"), None),
        P(("fsdp", "rep"), None),
        P(),
    )
    return jax.shard_map(
        shards,
        mesh=mesh,
        in_specs=placed,
        out_specs=(P("rep", "fsdp", None), P(("fsdp", "rep"), None), P(("fsdp", "rep"), None)),
        check_vma=False,
    )
```

```python
import math

import jax
import jax.numpy as jnp
from jax import lax
from jax.experimental import pallas as pl
from jax.experimental.pallas import tpu as pltpu
from jax.sharding import PartitionSpec as P

D = 8192
FRAG = 128
NFRAG = 4
HID = 512
NF = 8
NX = 4
NZ = 8
NQ = 16
ROWS = 128
HALF = ROWS // 2
DEPTH = D // NF
SHARE = 32
WIDE = 3 * FRAG
PAIR = 2 * FRAG
CHUNKS = 4
TILE = 256
PLACE = 512


INNER_RATE = 0.5
OUTER_RATE = 0.7
MOMENT = 0.9
MIX_RATE = 0.5
SCALE_IN = 1.0 / math.sqrt(D)
SCALE_HID = 1.0 / math.sqrt(HID)
BF16 = jnp.bfloat16
F32 = jnp.float32
MESH = pl.DeviceIdType.MESH


def dot(a, b):
    return jnp.dot(a, b, preferred_element_type=F32)


def step_kernel(
    tokens,
    cotangent,
    weights,
    global_ref,
    moment_ref,
    fragment,
    u_out,
    g_out,
    m_out,
    tcut,
    ccut,
    tturn,
    cturn,
    w,
    wrot,
    ysend,
    yrecv,
    far,
    near,
    psend,
    precv,
    prow,
    acts,
    u,
    u0,
    r1,
    s1,
    r2,
    gall,
    local_sem,
    a_send,
    a_recv,
    y_send,
    y_recv,
    h_send,
    h_recv,
    c_send,
    c_recv,
    s_send,
    s_recv,
    g_send,
    g_recv,
    t_send,
    t_recv,
    b_send,
    b_recv,
    entered,
):
    rep = lax.axis_index("rep")
    me = lax.axis_index("fsdp")
    x, yh = me % NX, me // NX
    core, q = rep % 2, rep // 2
    z, yl = q // 2, q % 2
    frag = lax.rem(fragment[0], NFRAG)

    def fsdp_to(k):
        return (x + k % NX) % NX + NX * ((yh + k // NX) % 2)

    def fsdp_from(k):
        return (x + NX - k % NX) % NX + NX * ((yh + k // NX) % 2)

    def q_to(k):
        return ((z + k // 2) % NZ) * 2 + (yl + k % 2) % 2

    def q_from(k):
        return ((z + NZ - k // 2) % NZ) * 2 + (yl + k % 2) % 2

    def at_fsdp(f):
        return (rep, f)

    def at_q(p):
        return (p * 2 + core, me)

    partner = (q * 2 + 1 - core, me)

    def each(n, body):
        def step(k, carry):
            body(k)
            return carry

        lax.fori_loop(0, n, step, 0)

    barrier = pltpu.get_barrier_semaphore()

    def greet_fsdp(i):
        pl.semaphore_signal(barrier, inc=1, device_id=at_fsdp(fsdp_to(i + 1)), device_id_type=MESH)

    def neighbour(dz, dy):
        return at_q((z + dz) % NZ * 2 + (yl + dy) % 2)

    def greet(sem, to):
        pl.semaphore_signal(sem, inc=1, device_id=to, device_id_type=MESH)

    each(NF - 1, greet_fsdp)
    greet(barrier, partner)
    greet(barrier, neighbour(0, 1))
    greet(barrier, neighbour(1, 0))
    greet(barrier, neighbour(NZ - 1, 0))

    own_cols = pl.ds(pl.multiple_of(me * DEPTH, DEPTH), DEPTH)
    own_rows = pl.ds(pl.multiple_of(me * ROWS, ROWS), ROWS)
    load_w = pltpu.make_async_copy(weights.at[0], w, local_sem.at[0])
    load_t = pltpu.make_async_copy(tokens.at[:, own_cols], tcut.at[own_rows], local_sem.at[1])
    load_c = pltpu.make_async_copy(cotangent.at[:, own_cols], ccut.at[own_rows], local_sem.at[2])
    load_w.start()
    load_t.start()
    load_c.start()
    pl.semaphore_wait(barrier, NF - 1 + 4)

    def all_of(block, send, recv):
        return pltpu.make_async_remote_copy(
            src_ref=block,
            dst_ref=block,
            send_sem=send,
            recv_sem=recv,
            device_id=partner,
            device_id_type=MESH,
        )

    others = pl.ds(0, (NF - 1) * ROWS)

    part = ROWS // CHUNKS

    def exchange(source, target, h, slot, k):
        f = fsdp_to(k)
        cols = pl.ds(pl.multiple_of(f * DEPTH, DEPTH), DEPTH)
        rows = pl.ds(pl.multiple_of(me * ROWS + h * part, part), part)
        return pltpu.make_async_remote_copy(
            src_ref=source.at[pl.ds(h * part, part), cols],
            dst_ref=target.at[rows],
            send_sem=a_send.at[slot],
            recv_sem=a_recv.at[slot],
            device_id=at_fsdp(f),
            device_id_type=MESH,
        )

    for h in range(CHUNKS):
        each(NF - 1, lambda i: exchange(tokens, tcut, h, 0, NF - 1 - i).start())
    for h in range(CHUNKS):
        each(NF - 1, lambda i: exchange(cotangent, ccut, h, 1, NF - 1 - i).start())

    for step in range(2):
        greet(entered.at[step], neighbour(1 + step, 0))
        greet(entered.at[step], neighbour(NZ - 1 - step, 0))
        pl.semaphore_wait(entered.at[step], 2)
    greet(entered.at[2], neighbour(0, 1))
    pl.semaphore_wait(entered.at[2], 1)

    load_w.wait()
    for j in range(NFRAG):
        first = lax.rem(frag + j, NFRAG) * FRAG
        for member in range(3):
            cols = pl.ds(first + member * HID, FRAG)
            wrot[j, :, member * FRAG : (member + 1) * FRAG] = w[:, cols]

    def tile_of(i):
        return pl.ds(pl.multiple_of(i * TILE, TILE), TILE)

    def spread(j, i, cols, value):
        block = value.astype(BF16).reshape(TILE // ROWS, ROWS, value.shape[-1])
        ysend[j, i // 2, pl.ds(i % 2 * 2, 2), :, cols] = block

    load_t.wait()
    all_of(tcut.at[others], a_send.at[0], a_recv.at[0]).wait_recv()

    def forward_t(i):
        rows = tcut[tile_of(i), :]
        for j in range(NFRAG):
            spread(j, i, slice(0, PAIR), dot(rows, wrot[j, :, :PAIR]) * SCALE_IN)
        tturn[:, tile_of(i)] = rows.T

    each(NF * ROWS // TILE, forward_t)

    lanes_of = (pl.ds(0, PAIR), pl.ds(PAIR, FRAG))

    def send_terms(k, at):
        f = fsdp_to(k)
        return pltpu.make_async_remote_copy(
            src_ref=ysend.at[0, f // NX, f % NX, :, lanes_of[at]],
            dst_ref=yrecv.at[k, :, lanes_of[at]],
            send_sem=y_send.at[at],
            recv_sem=y_recv.at[at],
            device_id=at_fsdp(f),
            device_id_type=MESH,
        )

    each(NF - 1, lambda i: send_terms(i + 1, 0).start())

    load_c.wait()
    all_of(ccut.at[others], a_send.at[1], a_recv.at[1]).wait_recv()

    def forward_c(groups):
        def run(i):
            rows = ccut[tile_of(i), :]
            for j in groups:
                spread(j, i, slice(PAIR, WIDE), dot(rows, wrot[j, :, PAIR:]) * SCALE_HID)

        return run

    def block_of(j, f):
        return acts.at[j, pl.ds(pl.multiple_of(f * ROWS, ROWS), ROWS)]

    def send_acts(k):
        block = block_of(0, me)
        return pltpu.make_async_remote_copy(
            src_ref=block,
            dst_ref=block,
            send_sem=h_send.at[0],
            recv_sem=h_recv.at[0],
            device_id=at_fsdp(fsdp_to(k)),
            device_id_type=MESH,
        )

    sent_terms = [
        all_of(yrecv.at[pl.ds(1, NF - 1), :, lanes_of[at]], y_send.at[at], y_recv.at[at])
        for at in range(2)
    ]
    sent_acts = all_of(acts.at[0, others], h_send.at[0], h_recv.at[0])

    ahead = ((x + 1) % NX, (x + 3) % NX)
    opposite = (x + 2) % NX
    beside = tuple(at_fsdp(at + NX * yh) for at in ahead)
    pole = at_fsdp(x + NX * (1 - yh))
    halves = (pl.ds(0, HALF), pl.ds(HALF, HALF))
    first_row = (1, 2)
    first_pole = (3,)

    def hop(source, target, sends, recvs, j, slot, to):
        return pltpu.make_async_remote_copy(
            src_ref=source,
            dst_ref=target,
            send_sem=sends.at[0],
            recv_sem=recvs.at[j - 1, slot],
            device_id=to,
            device_id_type=MESH,
        )

    def span_of(j):
        return pl.ds(yh, 1) if j in first_pole else pl.ds(0, 2)

    def seat_of(j):
        return pl.ds(0, 1) if j in first_pole else pl.ds(0, 2)

    def term_far(j, way):
        return hop(
            ysend.at[j, span_of(j), opposite, halves[way]],
            far.at[j - 1, way, seat_of(j)],
            t_send,
            t_recv,
            j,
            way,
            beside[way],
        )

    def term_near(j, way, late):
        half = halves[way if late else 1 - way]
        return hop(
            ysend.at[j, span_of(j), ahead[way], half],
            near.at[j - 1, way, seat_of(j), half],
            t_send,
            t_recv,
            j,
            2,
            beside[way],
        )

    def term_pole(j):
        if j in first_pole:
            return hop(ysend.at[j, 1 - yh], prow, t_send, t_recv, j, 3, pole)
        return hop(psend.at[j - 1], precv.at[j - 1], t_send, t_recv, j, 3, pole)

    def terms_far(j):
        for way in range(2):
            term_far(j, way).start()

    def terms_near(j):
        for way in range(2):
            term_near(j, way, 0).start()

    def terms_row_in(j):
        term_pole(j).wait_recv()
        ysend[j, yh] = (ysend[j, yh].astype(F32) + prow[...].astype(F32)).astype(BF16)

    def terms_pass(j):
        for way in range(2):
            term_far(j, way).wait_recv()
            own = ysend[j, span_of(j), ahead[way], halves[way]].astype(F32)
            sums = own + far[j - 1, way, seat_of(j)].astype(F32)
            ysend[j, span_of(j), ahead[way], halves[way]] = sums.astype(BF16)
            term_near(j, way, 1).start()

    def terms_got(j):
        all_of(near.at[j - 1, :, seat_of(j)], t_send.at[0], t_recv.at[j - 1, 2]).wait_recv()

    def terms_row(j, half, seat):
        total = ysend[j, half, x].astype(F32)
        for way in range(2):
            total = total + near[j - 1, way, seat].astype(F32)
        return total

    def terms_cross(j):
        terms_got(j)
        psend[j - 1] = terms_row(j, 1 - yh, 1 - yh).astype(BF16)
        term_pole(j).start()

    def terms_end(j):
        if j in first_pole:
            terms_got(j)
            activate(j, terms_row(j, yh, 0))
        else:
            term_pole(j).wait_recv()
            activate(j, terms_row(j, yh, yh) + precv[j - 1].astype(F32))

    def act_pole(j, f):
        return hop(block_of(j, f), block_of(j, f), b_send, b_recv, j, 0, pole)

    def act_near(j, way, other, at):
        block = block_of(j, at + NX * (1 - yh if other else yh))
        slot = 1 + way + 2 * other
        return hop(block, block, b_send, b_recv, j, slot, beside[way])

    def act_far(j, way, other, at):
        f = at + NX * (1 - yh if other else yh)
        rows = pl.ds(pl.multiple_of(f * ROWS + way * HALF, HALF), HALF)
        block = acts.at[j, rows]
        return hop(block, block, b_send, b_recv, j, 5, beside[way])

    def acts_begin(j):
        act_pole(j, me).start()
        for way in range(2):
            act_near(j, way, 0, x).start()

    def acts_turn(j):
        act_pole(j, x + NX * (1 - yh)).wait_recv()
        for way in range(2):
            act_near(j, way, 1, x).start()

    def acts_pass(j, other):
        for way in range(2):
            act_near(j, way, other, ahead[1 - way]).wait_recv()
            act_far(j, way, other, ahead[1 - way]).start()

    def acts_all(j, blocks, slot):
        return all_of(acts.at[j, pl.ds(0, blocks * ROWS)], b_send.at[0], b_recv.at[j - 1, slot])

    def acts_across(j):
        for way in range(2):
            act_near(j, way, 0, ahead[1 - way]).wait_recv()
            act_far(j, way, 0, ahead[1 - way]).start()
            act_pole(j, ahead[1 - way] + NX * yh).start()

    def acts_last(j):
        acts_all(j, 1, 5).wait_recv()
        act_pole(j, opposite + NX * yh).start()

    def acts_end(j):
        if j in first_pole:
            acts_all(j, NX, 0).wait_recv()
        else:
            acts_all(j, 2, 5).wait_recv()

    tiles = NF * ROWS // TILE
    each(tiles, forward_c((0,)))
    each(NF - 1, lambda i: send_terms(i + 1, 1).start())
    each(tiles, forward_c((1,)))
    terms_far(1)
    terms_near(1)
    each(tiles, forward_c((3,)))
    term_pole(3).start()
    each(tiles, forward_c((2,)))

    def turn_c(i):
        cturn[:, tile_of(i)] = ccut[tile_of(i), :].T

    each(tiles, turn_c)

    def activate(j, total):
        gate = total[:, :FRAG]
        up = total[:, FRAG:PAIR]
        hidden_grad = total[:, PAIR:]
        sigmoid = jax.nn.sigmoid(gate)
        silu = gate * sigmoid
        acts[j, own_rows, :FRAG] = (
            hidden_grad * up * sigmoid * (1.0 + gate * (1.0 - sigmoid))
        ).astype(BF16)
        acts[j, own_rows, FRAG:PAIR] = (hidden_grad * silu).astype(BF16)
        acts[j, own_rows, PAIR:] = (silu * up).astype(BF16)

    def descend(j, i):
        rows = tile_of(i)
        grad_in = dot(tturn[rows, :], acts[j, :, :PAIR]) * SCALE_IN
        grad_down = dot(cturn[rows, :], acts[j, :, PAIR:]) * SCALE_HID
        left = wrot[j, rows, :PAIR].astype(F32) - INNER_RATE * grad_in
        right = wrot[j, rows, PAIR:].astype(F32) - INNER_RATE * grad_down
        return left.astype(BF16), right.astype(BF16)

    for sent in sent_terms:
        sent.wait_recv()
    total = ysend[0, yh, x].astype(F32)
    for k in range(1, NF):
        total = total + yrecv[k].astype(F32)
    activate(0, total)
    each(NF - 1, lambda i: send_acts(i + 1).start())
    terms_pass(1)
    terms_far(2)
    terms_near(2)
    terms_row_in(3)
    terms_far(3)
    terms_pass(2)
    terms_near(3)
    sent_acts.wait_recv()

    span = TILE // (2 * SHARE)

    def descend_first(i):
        left, right = descend(0, i)
        at = pl.ds(i * span, span)
        u0[at, :, :, :PAIR] = left.reshape(span, 2, SHARE, PAIR)
        u0[at, :, :, PAIR:] = right.reshape(span, 2, SHARE, FRAG)

    each(DEPTH // TILE, descend_first)

    across = pltpu.make_async_remote_copy(
        src_ref=u0.at[:, 1 - core],
        dst_ref=r1,
        send_sem=c_send.at[0],
        recv_sem=c_recv.at[0],
        device_id=partner,
        device_id_type=MESH,
    )
    across.start()

    terms_cross(1)
    terms_pass(3)
    terms_cross(2)

    across.wait()
    s1[...] = (u0[:, core].astype(F32) + r1[...].astype(F32)).astype(BF16)

    def send_sum(k):
        p = q_to(k)
        return pltpu.make_async_remote_copy(
            src_ref=s1.at[p],
            dst_ref=r2.at[k],
            send_sem=s_send.at[0],
            recv_sem=s_recv.at[0],
            device_id=at_q(p),
            device_id_type=MESH,
        )

    each(NQ - 1, lambda i: send_sum(i + 1).start())
    for j in first_row + first_pole:
        terms_end(j)
        acts_begin(j)
    sent_sums = all_of(r2.at[pl.ds(1, NQ - 1)], s_send.at[0], s_recv.at[0])
    sent_sums.wait_recv()

    total = s1[q].astype(F32)
    for k in range(1, NQ):
        total = total + r2[k].astype(F32)
    first = frag * FRAG
    for member in range(3):
        cols = pl.ds(first + member * HID, FRAG)
        lanes = slice(member * FRAG, (member + 1) * FRAG)
        old = global_ref[:, cols].astype(F32)
        average = old - total[:, lanes] / (2 * NQ)
        moment = MOMENT * moment_ref[:, cols] + average
        m_out[:, lanes] = moment
        gall[q, core, :, lanes] = (old - OUTER_RATE * (average + MOMENT * moment)).astype(BF16)
    g_out[...] = gall[q, core]

    def send_global(k):
        block = gall.at[q, core]
        return pltpu.make_async_remote_copy(
            src_ref=block,
            dst_ref=block,
            send_sem=g_send.at[0],
            recv_sem=g_recv.at[0],
            device_id=at_q(q_to(k)),
            device_id_type=MESH,
        )

    sent_global = all_of(gall.at[pl.ds(0, NQ - 1), core], g_send.at[0], g_recv.at[0])
    each(NQ - 1, lambda i: send_global(i + 1).start())

    for j in first_row:
        acts_turn(j)
    for j in first_pole:
        acts_across(j)
    for j in first_row:
        acts_pass(j, 0)
    for j in first_pole:
        acts_last(j)
    for j in first_row:
        acts_pass(j, 1)

    def descend_rest(j):
        def run(i):
            left, right = descend(j, i)
            u[j, tile_of(i), :PAIR] = left
            u[j, tile_of(i), PAIR:] = right

        return run

    def store(j):
        return pltpu.make_async_copy(u.at[j], u_out.at[j], local_sem.at[3 + j])

    sent_global.wait_recv()
    side = gall.at[:, core]
    give = pltpu.make_async_remote_copy(
        src_ref=side,
        dst_ref=side,
        send_sem=c_send.at[1],
        recv_sem=c_recv.at[1],
        device_id=partner,
        device_id_type=MESH,
    )
    give.start()

    def finish(j):
        acts_end(j)
        each(DEPTH // TILE, descend_rest(j))
        store(j).start()

    finish(1)
    finish(2)
    give.wait_send()
    other = gall.at[:, 1 - core]
    pltpu.make_async_remote_copy(
        src_ref=other,
        dst_ref=other,
        send_sem=c_send.at[1],
        recv_sem=c_recv.at[1],
        device_id=partner,
        device_id_type=MESH,
    ).wait_recv()

    def mix(i):
        at = pl.ds(i * span, span)
        mixed = MIX_RATE * u0[at].astype(F32) + (1.0 - MIX_RATE) * gall[at].astype(F32)
        u[0, tile_of(i), :] = mixed.astype(BF16).reshape(TILE, WIDE)

    each(DEPTH // TILE, mix)
    store(0).start()
    finish(3)

    all_of(tcut.at[others], a_send.at[0], a_recv.at[0]).wait_send()
    all_of(ccut.at[others], a_send.at[1], a_recv.at[1]).wait_send()
    for sent in sent_terms:
        sent.wait_send()
    sent_acts.wait_send()
    every = acts.at[pl.ds(0, NFRAG - 1), others]
    all_of(every, t_send.at[0], t_recv.at[0, 0]).wait_send()
    all_of(every, b_send.at[0], b_recv.at[0, 0]).wait_send()
    sent_sums.wait_send()
    sent_global.wait_send()

    for j in range(NFRAG):
        store(j).wait()


def place_kernel(u, g, m, global_ref, moment_ref, fragment, w_out, g_out, m_out):
    frag = lax.rem(fragment[0], NFRAG)
    for at in range(NFRAG):
        j = lax.rem(at + NFRAG - frag, NFRAG)
        for member in range(3):
            cols = slice(member * HID + at * FRAG, member * HID + (at + 1) * FRAG)
            w_out[0, :, cols] = u[j, :, member * FRAG : (member + 1) * FRAG]

    @pl.when(pl.program_id(0) == 0)
    def _():
        for at in range(NFRAG):
            here = frag == at
            for member in range(3):
                cols = slice(member * HID + at * FRAG, member * HID + (at + 1) * FRAG)
                lanes = slice(member * FRAG, (member + 1) * FRAG)
                g_out[:, cols] = jnp.where(here, g[:, lanes], global_ref[:, cols])
                m_out[:, cols] = jnp.where(here, m[:, lanes], moment_ref[:, cols])


def shards(tokens, cotangent, weights, global_params, momentum, fragment):
    anywhere = pl.BlockSpec(memory_space=pl.ANY)
    vmem = pl.BlockSpec(memory_space=pltpu.VMEM)
    smem = pl.BlockSpec(memory_space=pltpu.SMEM)
    sem = pltpu.SemaphoreType.DMA
    u, g, m = pl.pallas_call(
        step_kernel,
        out_shape=(
            jax.ShapeDtypeStruct((NFRAG, DEPTH, WIDE), BF16),
            jax.ShapeDtypeStruct((SHARE, WIDE), BF16),
            jax.ShapeDtypeStruct((SHARE, WIDE), F32),
        ),
        in_specs=[anywhere, anywhere, anywhere, vmem, vmem, smem],
        out_specs=(anywhere, vmem, vmem),
        scratch_shapes=[
            pltpu.VMEM((NF * ROWS, DEPTH), BF16),
            pltpu.VMEM((NF * ROWS, DEPTH), BF16),
            pltpu.VMEM((DEPTH, NF * ROWS), BF16),
            pltpu.VMEM((DEPTH, NF * ROWS), BF16),
            pltpu.VMEM((DEPTH, 3 * HID), BF16),
            pltpu.VMEM((NFRAG, DEPTH, WIDE), BF16),
            pltpu.VMEM((NFRAG, 2, NX, ROWS, WIDE), BF16),
            pltpu.VMEM((NF, ROWS, WIDE), BF16),
            pltpu.VMEM((NFRAG - 1, 2, 2, HALF, WIDE), BF16),
            pltpu.VMEM((NFRAG - 1, 2, 2, ROWS, WIDE), BF16),
            pltpu.VMEM((NFRAG - 1, ROWS, WIDE), BF16),
            pltpu.VMEM((NFRAG - 1, ROWS, WIDE), BF16),
            pltpu.VMEM((NX, ROWS, WIDE), BF16),
            pltpu.VMEM((NFRAG, NF * ROWS, WIDE), BF16),
            pltpu.VMEM((NFRAG, DEPTH, WIDE), BF16),
            pltpu.VMEM((NQ, 2, SHARE, WIDE), BF16),
            pltpu.VMEM((NQ, SHARE, WIDE), BF16),
            pltpu.VMEM((NQ, SHARE, WIDE), BF16),
            pltpu.VMEM((NQ, SHARE, WIDE), BF16),
            pltpu.VMEM((NQ, 2, SHARE, WIDE), BF16),
            sem((3 + NFRAG,)),
            sem((2,)),
            sem((2,)),
            sem((2,)),
            sem((2,)),
            sem((1,)),
            sem((1,)),
            sem((2,)),
            sem((2,)),
            sem((1,)),
            sem((1,)),
            sem((1,)),
            sem((1,)),
            sem((1,)),
            sem((NFRAG - 1, 4)),
            sem((1,)),
            sem((NFRAG - 1, 6)),
            pltpu.SemaphoreType.REGULAR((3,)),
        ],
        compiler_params=pltpu.CompilerParams(
            collective_id=0, has_side_effects=True, vmem_limit_bytes=56 * 2**20
        ),
        cost_estimate=pl.CostEstimate(
            flops=4 * ROWS * D * 3 * HID, bytes_accessed=10 * 2**20, transcendentals=ROWS * HID
        ),
    )(tokens, cotangent, weights, global_params, momentum, fragment)
    return pl.pallas_call(
        place_kernel,
        out_shape=(
            jax.ShapeDtypeStruct((1, DEPTH, 3 * HID), BF16),
            jax.ShapeDtypeStruct(global_params.shape, BF16),
            jax.ShapeDtypeStruct(momentum.shape, F32),
        ),
        grid=(DEPTH // PLACE,),
        in_specs=[
            pl.BlockSpec((NFRAG, PLACE, WIDE), lambda i: (0, i, 0)),
            vmem,
            vmem,
            vmem,
            vmem,
            smem,
        ],
        out_specs=(pl.BlockSpec((1, PLACE, 3 * HID), lambda i: (0, i, 0)), vmem, vmem),
        cost_estimate=pl.CostEstimate(flops=0, bytes_accessed=6 * 2**20, transcendentals=0),
    )(u, g, m, global_params, momentum, fragment)


def solution(mesh):
    placed = (
        P(("rep", "fsdp"), None),
        P(("rep", "fsdp"), None),
        P("rep", "fsdp", None),
        P(("fsdp", "rep"), None),
        P(("fsdp", "rep"), None),
        P(),
    )
    return jax.shard_map(
        shards,
        mesh=mesh,
        in_specs=placed,
        out_specs=(P("rep", "fsdp", None), P(("fsdp", "rep"), None), P(("fsdp", "rep"), None)),
        check_vma=False,
    )
```

```python
import math

import jax
import jax.numpy as jnp
from jax import lax
from jax.experimental import pallas as pl
from jax.experimental.pallas import tpu as pltpu
from jax.sharding import PartitionSpec as P

D = 8192
FRAG = 128
NFRAG = 4
HID = 512
NF = 8
NX = 4
NZ = 8
NQ = 16
ROWS = 128
HALF = ROWS // 2
DEPTH = D // NF
SHARE = 32
WIDE = 3 * FRAG
PAIR = 2 * FRAG
CHUNKS = 4
TILE = 256
PLACE = 512


INNER_RATE = 0.5
OUTER_RATE = 0.7
MOMENT = 0.9
MIX_RATE = 0.5
SCALE_IN = 1.0 / math.sqrt(D)
SCALE_HID = 1.0 / math.sqrt(HID)
BF16 = jnp.bfloat16
F32 = jnp.float32
MESH = pl.DeviceIdType.MESH


def dot(a, b):
    return jnp.dot(a, b, preferred_element_type=F32)


def step_kernel(
    tokens,
    cotangent,
    weights,
    global_ref,
    moment_ref,
    fragment,
    u_out,
    g_out,
    m_out,
    tcut,
    ccut,
    tturn,
    cturn,
    w,
    wrot,
    ysend,
    yrecv,
    far,
    near,
    psend,
    precv,
    prow,
    acts,
    u,
    u0,
    r1,
    s1,
    r2,
    gall,
    local_sem,
    a_send,
    a_recv,
    y_send,
    y_recv,
    h_send,
    h_recv,
    c_send,
    c_recv,
    s_send,
    s_recv,
    g_send,
    g_recv,
    t_send,
    t_recv,
    b_send,
    b_recv,
    entered,
):
    rep = lax.axis_index("rep")
    me = lax.axis_index("fsdp")
    x, yh = me % NX, me // NX
    core, q = rep % 2, rep // 2
    z, yl = q // 2, q % 2
    frag = lax.rem(fragment[0], NFRAG)

    def fsdp_to(k):
        return (x + k % NX) % NX + NX * ((yh + k // NX) % 2)

    def fsdp_from(k):
        return (x + NX - k % NX) % NX + NX * ((yh + k // NX) % 2)

    def q_to(k):
        return ((z + k // 2) % NZ) * 2 + (yl + k % 2) % 2

    def q_from(k):
        return ((z + NZ - k // 2) % NZ) * 2 + (yl + k % 2) % 2

    def at_fsdp(f):
        return (rep, f)

    def at_q(p):
        return (p * 2 + core, me)

    partner = (q * 2 + 1 - core, me)

    def each(n, body):
        def step(k, carry):
            body(k)
            return carry

        lax.fori_loop(0, n, step, 0)

    barrier = pltpu.get_barrier_semaphore()

    def neighbour(dz, dy):
        return at_q((z + dz) % NZ * 2 + (yl + dy) % 2)

    def greet(sem, to):
        pl.semaphore_signal(sem, inc=1, device_id=to, device_id_type=MESH)

    nearest = [at_fsdp(fsdp_to(k)) for k in (1, 3, 4)]
    for to in nearest:
        greet(barrier, to)
    greet(barrier, partner)
    greet(barrier, neighbour(0, 1))
    greet(barrier, neighbour(1, 0))
    greet(barrier, neighbour(NZ - 1, 0))

    own_cols = pl.ds(pl.multiple_of(me * DEPTH, DEPTH), DEPTH)
    own_rows = pl.ds(pl.multiple_of(me * ROWS, ROWS), ROWS)
    load_w = pltpu.make_async_copy(weights.at[0], w, local_sem.at[0])
    load_t = pltpu.make_async_copy(tokens.at[:, own_cols], tcut.at[own_rows], local_sem.at[1])
    load_c = pltpu.make_async_copy(cotangent.at[:, own_cols], ccut.at[own_rows], local_sem.at[2])
    load_w.start()
    load_t.start()
    load_c.start()
    pl.semaphore_wait(barrier, 3 + 4)

    def all_of(block, send, recv):
        return pltpu.make_async_remote_copy(
            src_ref=block,
            dst_ref=block,
            send_sem=send,
            recv_sem=recv,
            device_id=partner,
            device_id_type=MESH,
        )

    others = pl.ds(0, (NF - 1) * ROWS)

    part = ROWS // CHUNKS

    def exchange(source, target, h, slot, k):
        f = fsdp_to(k)
        cols = pl.ds(pl.multiple_of(f * DEPTH, DEPTH), DEPTH)
        rows = pl.ds(pl.multiple_of(me * ROWS + h * part, part), part)
        return pltpu.make_async_remote_copy(
            src_ref=source.at[pl.ds(h * part, part), cols],
            dst_ref=target.at[rows],
            send_sem=a_send.at[slot],
            recv_sem=a_recv.at[slot],
            device_id=at_fsdp(f),
            device_id_type=MESH,
        )

    for k in (4, 1, 3):
        exchange(tokens, tcut, 0, 0, k).start()
    for to in nearest:
        greet(entered.at[3], to)
    pl.semaphore_wait(entered.at[3], 3)
    greet(entered.at[4], nearest[1])
    for k in (5, 7, 2):
        exchange(tokens, tcut, 0, 0, k).start()
    pl.semaphore_wait(entered.at[4], 1)
    exchange(tokens, tcut, 0, 0, 6).start()
    for h in range(1, CHUNKS):
        each(NF - 1, lambda i: exchange(tokens, tcut, h, 0, NF - 1 - i).start())
    for h in range(CHUNKS):
        each(NF - 1, lambda i: exchange(cotangent, ccut, h, 1, NF - 1 - i).start())

    for step in range(2):
        greet(entered.at[step], neighbour(1 + step, 0))
        greet(entered.at[step], neighbour(NZ - 1 - step, 0))
        pl.semaphore_wait(entered.at[step], 2)
    greet(entered.at[2], neighbour(0, 1))
    pl.semaphore_wait(entered.at[2], 1)

    load_w.wait()
    for j in range(NFRAG):
        first = lax.rem(frag + j, NFRAG) * FRAG
        for member in range(3):
            cols = pl.ds(first + member * HID, FRAG)
            wrot[j, :, member * FRAG : (member + 1) * FRAG] = w[:, cols]

    def tile_of(i):
        return pl.ds(pl.multiple_of(i * TILE, TILE), TILE)

    def spread(j, i, cols, value):
        block = value.astype(BF16).reshape(TILE // ROWS, ROWS, value.shape[-1])
        ysend[j, i // 2, pl.ds(i % 2 * 2, 2), :, cols] = block

    load_t.wait()
    all_of(tcut.at[others], a_send.at[0], a_recv.at[0]).wait_recv()

    def forward_t(i):
        rows = tcut[tile_of(i), :]
        for j in range(NFRAG):
            spread(j, i, slice(0, PAIR), dot(rows, wrot[j, :, :PAIR]) * SCALE_IN)
        tturn[:, tile_of(i)] = rows.T

    each(NF * ROWS // TILE, forward_t)

    lanes_of = (pl.ds(0, PAIR), pl.ds(PAIR, FRAG))

    def send_terms(k, at):
        f = fsdp_to(k)
        return pltpu.make_async_remote_copy(
            src_ref=ysend.at[0, f // NX, f % NX, :, lanes_of[at]],
            dst_ref=yrecv.at[k, :, lanes_of[at]],
            send_sem=y_send.at[at],
            recv_sem=y_recv.at[at],
            device_id=at_fsdp(f),
            device_id_type=MESH,
        )

    each(NF - 1, lambda i: send_terms(i + 1, 0).start())

    load_c.wait()
    all_of(ccut.at[others], a_send.at[1], a_recv.at[1]).wait_recv()

    def forward_c(groups):
        def run(i):
            rows = ccut[tile_of(i), :]
            for j in groups:
                spread(j, i, slice(PAIR, WIDE), dot(rows, wrot[j, :, PAIR:]) * SCALE_HID)

        return run

    def block_of(j, f):
        return acts.at[j, pl.ds(pl.multiple_of(f * ROWS, ROWS), ROWS)]

    def send_acts(k):
        block = block_of(0, me)
        return pltpu.make_async_remote_copy(
            src_ref=block,
            dst_ref=block,
            send_sem=h_send.at[0],
            recv_sem=h_recv.at[0],
            device_id=at_fsdp(fsdp_to(k)),
            device_id_type=MESH,
        )

    sent_terms = [
        all_of(yrecv.at[pl.ds(1, NF - 1), :, lanes_of[at]], y_send.at[at], y_recv.at[at])
        for at in range(2)
    ]
    sent_acts = all_of(acts.at[0, others], h_send.at[0], h_recv.at[0])

    ahead = ((x + 1) % NX, (x + 3) % NX)
    opposite = (x + 2) % NX
    beside = tuple(at_fsdp(at + NX * yh) for at in ahead)
    pole = at_fsdp(x + NX * (1 - yh))
    halves = (pl.ds(0, HALF), pl.ds(HALF, HALF))
    first_row = (1, 2)
    first_pole = (3,)

    def hop(source, target, sends, recvs, j, slot, to):
        return pltpu.make_async_remote_copy(
            src_ref=source,
            dst_ref=target,
            send_sem=sends.at[0],
            recv_sem=recvs.at[j - 1, slot],
            device_id=to,
            device_id_type=MESH,
        )

    def span_of(j):
        return pl.ds(yh, 1) if j in first_pole else pl.ds(0, 2)

    def seat_of(j):
        return pl.ds(0, 1) if j in first_pole else pl.ds(0, 2)

    def term_far(j, way):
        return hop(
            ysend.at[j, span_of(j), opposite, halves[way]],
            far.at[j - 1, way, seat_of(j)],
            t_send,
            t_recv,
            j,
            way,
            beside[way],
        )

    def term_near(j, way, late):
        half = halves[way if late else 1 - way]
        return hop(
            ysend.at[j, span_of(j), ahead[way], half],
            near.at[j - 1, way, seat_of(j), half],
            t_send,
            t_recv,
            j,
            2,
            beside[way],
        )

    def term_pole(j):
        if j in first_pole:
            return hop(ysend.at[j, 1 - yh], prow, t_send, t_recv, j, 3, pole)
        return hop(psend.at[j - 1], precv.at[j - 1], t_send, t_recv, j, 3, pole)

    def terms_far(j):
        for way in range(2):
            term_far(j, way).start()

    def terms_near(j):
        for way in range(2):
            term_near(j, way, 0).start()

    def terms_row_in(j):
        term_pole(j).wait_recv()
        ysend[j, yh] = (ysend[j, yh].astype(F32) + prow[...].astype(F32)).astype(BF16)

    def terms_pass(j):
        for way in range(2):
            term_far(j, way).wait_recv()
            own = ysend[j, span_of(j), ahead[way], halves[way]].astype(F32)
            sums = own + far[j - 1, way, seat_of(j)].astype(F32)
            ysend[j, span_of(j), ahead[way], halves[way]] = sums.astype(BF16)
            term_near(j, way, 1).start()

    def terms_got(j):
        all_of(near.at[j - 1, :, seat_of(j)], t_send.at[0], t_recv.at[j - 1, 2]).wait_recv()

    def terms_row(j, half, seat):
        total = ysend[j, half, x].astype(F32)
        for way in range(2):
            total = total + near[j - 1, way, seat].astype(F32)
        return total

    def terms_cross(j):
        terms_got(j)
        psend[j - 1] = terms_row(j, 1 - yh, 1 - yh).astype(BF16)
        term_pole(j).start()

    def terms_end(j):
        if j in first_pole:
            terms_got(j)
            activate(j, terms_row(j, yh, 0))
        else:
            term_pole(j).wait_recv()
            activate(j, terms_row(j, yh, yh) + precv[j - 1].astype(F32))

    def act_pole(j, f):
        return hop(block_of(j, f), block_of(j, f), b_send, b_recv, j, 0, pole)

    def act_near(j, way, other, at):
        block = block_of(j, at + NX * (1 - yh if other else yh))
        slot = 1 + way + 2 * other
        return hop(block, block, b_send, b_recv, j, slot, beside[way])

    def act_far(j, way, other, at):
        f = at + NX * (1 - yh if other else yh)
        rows = pl.ds(pl.multiple_of(f * ROWS + way * HALF, HALF), HALF)
        block = acts.at[j, rows]
        return hop(block, block, b_send, b_recv, j, 5, beside[way])

    def acts_begin(j):
        act_pole(j, me).start()
        for way in range(2):
            act_near(j, way, 0, x).start()

    def acts_turn(j):
        act_pole(j, x + NX * (1 - yh)).wait_recv()
        for way in range(2):
            act_near(j, way, 1, x).start()

    def acts_pass(j, other):
        for way in range(2):
            act_near(j, way, other, ahead[1 - way]).wait_recv()
            act_far(j, way, other, ahead[1 - way]).start()

    def acts_all(j, blocks, slot):
        return all_of(acts.at[j, pl.ds(0, blocks * ROWS)], b_send.at[0], b_recv.at[j - 1, slot])

    def acts_across(j):
        for way in range(2):
            act_near(j, way, 0, ahead[1 - way]).wait_recv()
            act_far(j, way, 0, ahead[1 - way]).start()
            act_pole(j, ahead[1 - way] + NX * yh).start()

    def acts_last(j):
        acts_all(j, 1, 5).wait_recv()
        act_pole(j, opposite + NX * yh).start()

    def acts_end(j):
        if j in first_pole:
            acts_all(j, NX, 0).wait_recv()
        else:
            acts_all(j, 2, 5).wait_recv()

    tiles = NF * ROWS // TILE
    each(tiles, forward_c((0,)))
    for k in range(NF - 1, 0, -1):
        send_terms(k, 1).start()
    each(tiles, forward_c((1,)))
    terms_far(1)
    terms_near(1)
    each(tiles, forward_c((3,)))
    term_pole(3).start()
    each(tiles, forward_c((2,)))

    def turn_c(i):
        cturn[:, tile_of(i)] = ccut[tile_of(i), :].T

    each(tiles, turn_c)

    def activate(j, total):
        gate = total[:, :FRAG]
        up = total[:, FRAG:PAIR]
        hidden_grad = total[:, PAIR:]
        sigmoid = jax.nn.sigmoid(gate)
        silu = gate * sigmoid
        acts[j, own_rows, :FRAG] = (
            hidden_grad * up * sigmoid * (1.0 + gate * (1.0 - sigmoid))
        ).astype(BF16)
        acts[j, own_rows, FRAG:PAIR] = (hidden_grad * silu).astype(BF16)
        acts[j, own_rows, PAIR:] = (silu * up).astype(BF16)

    def descend(j, i):
        rows = tile_of(i)
        grad_in = dot(tturn[rows, :], acts[j, :, :PAIR]) * SCALE_IN
        grad_down = dot(cturn[rows, :], acts[j, :, PAIR:]) * SCALE_HID
        left = wrot[j, rows, :PAIR].astype(F32) - INNER_RATE * grad_in
        right = wrot[j, rows, PAIR:].astype(F32) - INNER_RATE * grad_down
        return left.astype(BF16), right.astype(BF16)

    for sent in sent_terms:
        sent.wait_recv()
    total = ysend[0, yh, x].astype(F32)
    for k in range(1, NF):
        total = total + yrecv[k].astype(F32)
    activate(0, total)
    for k in range(NF - 1, 0, -1):
        send_acts(k).start()
    terms_pass(1)
    terms_far(2)
    terms_near(2)
    terms_row_in(3)
    terms_far(3)
    terms_pass(2)
    terms_near(3)
    sent_acts.wait_recv()

    span = TILE // (2 * SHARE)

    def descend_first(i):
        left, right = descend(0, i)
        at = pl.ds(i * span, span)
        u0[at, :, :, :PAIR] = left.reshape(span, 2, SHARE, PAIR)
        u0[at, :, :, PAIR:] = right.reshape(span, 2, SHARE, FRAG)

    each(DEPTH // TILE, descend_first)

    across = pltpu.make_async_remote_copy(
        src_ref=u0.at[:, 1 - core],
        dst_ref=r1,
        send_sem=c_send.at[0],
        recv_sem=c_recv.at[0],
        device_id=partner,
        device_id_type=MESH,
    )
    across.start()

    terms_cross(1)
    across.wait()
    s1[...] = (u0[:, core].astype(F32) + r1[...].astype(F32)).astype(BF16)

    far_first = (8, 9, 7, 11, 6, 10, 5, 13, 4, 12, 3, 15, 2, 14, 1)

    def send_sum(k):
        p = q_to(k)
        return pltpu.make_async_remote_copy(
            src_ref=s1.at[p],
            dst_ref=r2.at[k],
            send_sem=s_send.at[0],
            recv_sem=s_recv.at[0],
            device_id=at_q(p),
            device_id_type=MESH,
        )

    for k in far_first:
        send_sum(k).start()
    terms_pass(3)
    terms_cross(2)

    for j in first_row + first_pole:
        terms_end(j)
        acts_begin(j)
    sent_sums = all_of(r2.at[pl.ds(1, NQ - 1)], s_send.at[0], s_recv.at[0])
    sent_sums.wait_recv()

    total = s1[q].astype(F32)
    for k in range(1, NQ):
        total = total + r2[k].astype(F32)
    first = frag * FRAG
    for member in range(3):
        cols = pl.ds(first + member * HID, FRAG)
        lanes = slice(member * FRAG, (member + 1) * FRAG)
        old = global_ref[:, cols].astype(F32)
        average = old - total[:, lanes] / (2 * NQ)
        moment = MOMENT * moment_ref[:, cols] + average
        m_out[:, lanes] = moment
        gall[q, core, :, lanes] = (old - OUTER_RATE * (average + MOMENT * moment)).astype(BF16)
    g_out[...] = gall[q, core]

    def send_global(k):
        block = gall.at[q, core]
        return pltpu.make_async_remote_copy(
            src_ref=block,
            dst_ref=block,
            send_sem=g_send.at[0],
            recv_sem=g_recv.at[0],
            device_id=at_q(q_to(k)),
            device_id_type=MESH,
        )

    sent_global = all_of(gall.at[pl.ds(0, NQ - 1), core], g_send.at[0], g_recv.at[0])
    for k in far_first:
        send_global(k).start()

    for j in first_row:
        acts_turn(j)
    for j in first_pole:
        acts_across(j)
    for j in first_row:
        acts_pass(j, 0)
    for j in first_pole:
        acts_last(j)
    for j in first_row:
        acts_pass(j, 1)

    def descend_rest(j):
        def run(i):
            left, right = descend(j, i)
            u[j, tile_of(i), :PAIR] = left
            u[j, tile_of(i), PAIR:] = right

        return run

    def store(j):
        return pltpu.make_async_copy(u.at[j], u_out.at[j], local_sem.at[3 + j])

    sent_global.wait_recv()
    side = gall.at[:, core]
    give = pltpu.make_async_remote_copy(
        src_ref=side,
        dst_ref=side,
        send_sem=c_send.at[1],
        recv_sem=c_recv.at[1],
        device_id=partner,
        device_id_type=MESH,
    )
    give.start()

    def finish(j):
        acts_end(j)
        each(DEPTH // TILE, descend_rest(j))
        store(j).start()

    finish(1)
    finish(2)
    give.wait_send()
    other = gall.at[:, 1 - core]
    pltpu.make_async_remote_copy(
        src_ref=other,
        dst_ref=other,
        send_sem=c_send.at[1],
        recv_sem=c_recv.at[1],
        device_id=partner,
        device_id_type=MESH,
    ).wait_recv()

    def mix(i):
        at = pl.ds(i * span, span)
        mixed = MIX_RATE * u0[at].astype(F32) + (1.0 - MIX_RATE) * gall[at].astype(F32)
        u[0, tile_of(i), :] = mixed.astype(BF16).reshape(TILE, WIDE)

    each(DEPTH // TILE, mix)
    store(0).start()
    finish(3)

    all_of(tcut.at[others], a_send.at[0], a_recv.at[0]).wait_send()
    all_of(ccut.at[others], a_send.at[1], a_recv.at[1]).wait_send()
    for sent in sent_terms:
        sent.wait_send()
    sent_acts.wait_send()
    every = acts.at[pl.ds(0, NFRAG - 1), others]
    all_of(every, t_send.at[0], t_recv.at[0, 0]).wait_send()
    all_of(every, b_send.at[0], b_recv.at[0, 0]).wait_send()
    sent_sums.wait_send()
    sent_global.wait_send()

    for j in range(NFRAG):
        store(j).wait()


def place_kernel(u, g, m, global_ref, moment_ref, fragment, w_out, g_out, m_out):
    frag = lax.rem(fragment[0], NFRAG)
    for at in range(NFRAG):
        j = lax.rem(at + NFRAG - frag, NFRAG)
        for member in range(3):
            cols = slice(member * HID + at * FRAG, member * HID + (at + 1) * FRAG)
            w_out[0, :, cols] = u[j, :, member * FRAG : (member + 1) * FRAG]

    @pl.when(pl.program_id(0) == 0)
    def _():
        for at in range(NFRAG):
            here = frag == at
            for member in range(3):
                cols = slice(member * HID + at * FRAG, member * HID + (at + 1) * FRAG)
                lanes = slice(member * FRAG, (member + 1) * FRAG)
                g_out[:, cols] = jnp.where(here, g[:, lanes], global_ref[:, cols])
                m_out[:, cols] = jnp.where(here, m[:, lanes], moment_ref[:, cols])


def shards(tokens, cotangent, weights, global_params, momentum, fragment):
    anywhere = pl.BlockSpec(memory_space=pl.ANY)
    vmem = pl.BlockSpec(memory_space=pltpu.VMEM)
    smem = pl.BlockSpec(memory_space=pltpu.SMEM)
    sem = pltpu.SemaphoreType.DMA
    u, g, m = pl.pallas_call(
        step_kernel,
        out_shape=(
            jax.ShapeDtypeStruct((NFRAG, DEPTH, WIDE), BF16),
            jax.ShapeDtypeStruct((SHARE, WIDE), BF16),
            jax.ShapeDtypeStruct((SHARE, WIDE), F32),
        ),
        in_specs=[anywhere, anywhere, anywhere, vmem, vmem, smem],
        out_specs=(anywhere, vmem, vmem),
        scratch_shapes=[
            pltpu.VMEM((NF * ROWS, DEPTH), BF16),
            pltpu.VMEM((NF * ROWS, DEPTH), BF16),
            pltpu.VMEM((DEPTH, NF * ROWS), BF16),
            pltpu.VMEM((DEPTH, NF * ROWS), BF16),
            pltpu.VMEM((DEPTH, 3 * HID), BF16),
            pltpu.VMEM((NFRAG, DEPTH, WIDE), BF16),
            pltpu.VMEM((NFRAG, 2, NX, ROWS, WIDE), BF16),
            pltpu.VMEM((NF, ROWS, WIDE), BF16),
            pltpu.VMEM((NFRAG - 1, 2, 2, HALF, WIDE), BF16),
            pltpu.VMEM((NFRAG - 1, 2, 2, ROWS, WIDE), BF16),
            pltpu.VMEM((NFRAG - 1, ROWS, WIDE), BF16),
            pltpu.VMEM((NFRAG - 1, ROWS, WIDE), BF16),
            pltpu.VMEM((NX, ROWS, WIDE), BF16),
            pltpu.VMEM((NFRAG, NF * ROWS, WIDE), BF16),
            pltpu.VMEM((NFRAG, DEPTH, WIDE), BF16),
            pltpu.VMEM((NQ, 2, SHARE, WIDE), BF16),
            pltpu.VMEM((NQ, SHARE, WIDE), BF16),
            pltpu.VMEM((NQ, SHARE, WIDE), BF16),
            pltpu.VMEM((NQ, SHARE, WIDE), BF16),
            pltpu.VMEM((NQ, 2, SHARE, WIDE), BF16),
            sem((3 + NFRAG,)),
            sem((2,)),
            sem((2,)),
            sem((2,)),
            sem((2,)),
            sem((1,)),
            sem((1,)),
            sem((2,)),
            sem((2,)),
            sem((1,)),
            sem((1,)),
            sem((1,)),
            sem((1,)),
            sem((1,)),
            sem((NFRAG - 1, 4)),
            sem((1,)),
            sem((NFRAG - 1, 6)),
            pltpu.SemaphoreType.REGULAR((5,)),
        ],
        compiler_params=pltpu.CompilerParams(
            collective_id=0, has_side_effects=True, vmem_limit_bytes=56 * 2**20
        ),
        cost_estimate=pl.CostEstimate(
            flops=4 * ROWS * D * 3 * HID, bytes_accessed=10 * 2**20, transcendentals=ROWS * HID
        ),
    )(tokens, cotangent, weights, global_params, momentum, fragment)
    return pl.pallas_call(
        place_kernel,
        out_shape=(
            jax.ShapeDtypeStruct((1, DEPTH, 3 * HID), BF16),
            jax.ShapeDtypeStruct(global_params.shape, BF16),
            jax.ShapeDtypeStruct(momentum.shape, F32),
        ),
        grid=(DEPTH // PLACE,),
        in_specs=[
            pl.BlockSpec((NFRAG, PLACE, WIDE), lambda i: (0, i, 0)),
            vmem,
            vmem,
            vmem,
            vmem,
            smem,
        ],
        out_specs=(pl.BlockSpec((1, PLACE, 3 * HID), lambda i: (0, i, 0)), vmem, vmem),
        cost_estimate=pl.CostEstimate(flops=0, bytes_accessed=6 * 2**20, transcendentals=0),
    )(u, g, m, global_params, momentum, fragment)


def solution(mesh):
    placed = (
        P(("rep", "fsdp"), None),
        P(("rep", "fsdp"), None),
        P("rep", "fsdp", None),
        P(("fsdp", "rep"), None),
        P(("fsdp", "rep"), None),
        P(),
    )
    return jax.shard_map(
        shards,
        mesh=mesh,
        in_specs=placed,
        out_specs=(P("rep", "fsdp", None), P(("fsdp", "rep"), None), P(("fsdp", "rep"), None)),
        check_vma=False,
    )
```
